32 devices in a mesh: gx: 4 (over y, x), gy: 8 (over z, core).
Axes of the slice: x: 2, y: 2, z: 4, core: 2. Of those that a mesh axis runs over, the one named last changes fastest.
Arguments:
- features: bfloat16 [4, 8, 1, 192, 512], P('gx', 'gy'), may hold values from -6 to 6
- occupancy: int32 [4, 8, 1, 512], P('gx', 'gy'), may hold values 0 or 1
- brick_pos: int32 [4, 8, 1], P('gx', 'gy'), may hold values from 0 to 3, as said below
- weight: bfloat16 [192, 27, 192], replicated, may hold values from -0.125 to 0.125
- cotangent: bfloat16 [4, 8, 1, 192, 512], P('gx', 'gy'), may hold values from -6 to 6
Outputs:
- output: bfloat16 [4, 8, 1, 192, 512], P('gx', 'gy')
- x_grad: bfloat16 [4, 8, 1, 192, 512], P('gx', 'gy')
- w_grad: float32 [192, 27, 192], P('gx', None, 'gy')
The draws below stay inside these ranges and needn't reach their ends.
Inputs may be any that keep to these rules, and one draw needn't show every extreme that they name: `brick_pos`: the 1 positions of one device are distinct.
All inputs are finite; a program needn't handle non-finite values. No bound on the sum of `occupancy` on one device may be relied on, other than what follows from the above.
Results may differ from the reference program's by a relative error of at most 0.014.
Values may be sent and summed in bfloat16 or wider, within the bound.
No kernel may reach another device: no remote copies, remote signals or barrier semaphores. Data moves between devices by JAX's collectives and lax.ppermute only.
A program may use at most 64 MiB of HBM per device.

```python
import jax
import jax.numpy as jnp
from jax import lax

C = 192
BE = 8
VOX = 512
TX = 2
TY = 2
S = 1
HZ = 1
BRICKS = 32
N_GX = 4
N_GY = 8


def draw_brick_pos(key, part):
    spot_count = TX * TY * HZ
    scores = jax.random.randint(key, (N_GX, N_GY, spot_count), 0, 1048576) * spot_count + jnp.arange(spot_count, dtype=jnp.int32)
    scores = scores.at[0, 0, spot_count - 1].set(-1)
    scores = scores.at[N_GX - 1, N_GY - 1, 0].set(-1)
    ranking = jnp.argsort(scores, axis=-1, stable=True)
    return ranking[:, :, :S].astype(jnp.int32)


def plant(entries, key, smallest, largest):
    place = [jax.random.randint(jax.random.fold_in(key, axis), (), 0, length) for axis, length in enumerate(entries.shape)]
    main_axis = entries.shape.index(max(entries.shape))
    next_to = place[:main_axis] + [(place[main_axis] + 1) % entries.shape[main_axis]] + place[main_axis + 1:]
    return entries.at[tuple(place)].set(smallest).at[tuple(next_to)].set(largest)


def shard_levels(rng, shape, shards, least, high):
    level = 1.0
    for position, parts in shards:
        draws = jax.random.uniform(jax.random.fold_in(jax.random.fold_in(rng, 6), position), (parts,), jnp.float32, least / len(shards), high / len(shards))
        level = level * jnp.repeat(jnp.exp(draws), shape[position] // parts).reshape((-1,) + (1,) * (len(shape) - 1 - position))
    return level


def scatter_about(own_key, shape, deviation, most, cuts=(), kind=jnp.bfloat16):
    gain = shard_levels(own_key, shape, cuts, -0.22, 0.18) if cuts else 1.0
    drawn = jax.random.normal(own_key, shape, jnp.float32) * deviation * gain
    return jnp.minimum(jnp.maximum(drawn, -most), most).astype(kind)


def setup_inputs(seed: int = 0) -> dict:
    seeds = jax.random.split(jax.random.key(seed), 6)
    return {
        "features": scatter_about(seeds[0], (N_GX, N_GY, S, C, VOX), 1.0, 6.0, ((0, 4), (1, 8))),
        "occupancy": plant((jax.random.randint(seeds[1], (N_GX, N_GY, S, VOX), 0, 2) < 1).astype(jnp.int32), jax.random.fold_in(seeds[1], 1), 0, 1),
        "brick_pos": draw_brick_pos(jax.random.fold_in(seeds[5], 71), 0),
        "weight": scatter_about(seeds[3], (C, 27, C), (27 * C // 2) ** -0.5, 0.125),
        "cotangent": scatter_about(seeds[4], (N_GX, N_GY, S, C, VOX), 1.0, 6.0, ((0, 4), (1, 8))),
    }


def tap_windows(window, flipped):
    channels = window.shape[0]
    pieces = []
    for tap_x in range(3):
        for tap_y in range(3):
            for tap_z in range(3):
                if flipped:
                    start_x, start_y, start_z = 2 - tap_x, 2 - tap_y, 2 - tap_z
                else:
                    start_x, start_y, start_z = tap_x, tap_y, tap_z
                piece_view = window[:, start_x:start_x + BE, start_y:start_y + BE, start_z:start_z + BE]
                pieces.append(piece_view.reshape(channels, BE * BE * BE))
    return jnp.stack(pieces, axis=0)


def build_lattice(bricks, brick_x, brick_y, brick_z):
    rows_x, rows_y, slot_count, channels, voxels = bricks.shape
    holder = jnp.zeros((rows_x * TX, rows_y * TY, HZ, channels, BE, BE, BE), bricks.dtype)
    holder = holder.at[brick_x, brick_y, brick_z].set(bricks.reshape(rows_x, rows_y, slot_count, channels, BE, BE, BE))
    lattice = holder.transpose(3, 0, 4, 1, 5, 2, 6).reshape(channels, rows_x * TX * BE, rows_y * TY * BE, HZ * BE)
    return jnp.pad(lattice, ((0, 0), (1, 1), (1, 1), (1, 1)))


def silu_slope(values_in):
    sigma = jax.nn.sigmoid(values_in)
    return sigma * (1.0 + values_in * (1.0 - sigma))


def reference(features, occupancy, brick_pos, weight, cotangent):
    rows_x, rows_y, slot_count, channels, voxels = features.shape
    total = rows_x * rows_y * slot_count
    live_mask = occupancy.astype(jnp.bfloat16)[:, :, :, None, :]
    masked = features * live_mask
    brick_x = (brick_pos // (TY * HZ) + (jnp.arange(rows_x, dtype=jnp.int32) * TX)[:, None, None]).astype(jnp.int32)
    brick_y = ((brick_pos // HZ) % TY + (jnp.arange(rows_y, dtype=jnp.int32) * TY)[None, :, None]).astype(jnp.int32)
    brick_z = (brick_pos % HZ).astype(jnp.int32)
    start_x = (brick_x * BE).reshape(total).astype(jnp.int32)
    start_y = (brick_y * BE).reshape(total).astype(jnp.int32)
    start_z = (brick_z * BE).reshape(total).astype(jnp.int32)
    zero_idx = jnp.zeros((), jnp.int32)
    lattice = build_lattice(masked, brick_x, brick_y, brick_z)
    flat_weight = weight.reshape(channels, 27 * channels)

    def forward_one(brick_index):
        window = lax.dynamic_slice(lattice, (zero_idx, start_x[brick_index], start_y[brick_index], start_z[brick_index]), (channels, BE + 2, BE + 2, BE + 2))
        columns = tap_windows(window, False).reshape(27 * channels, voxels)
        return jnp.dot(flat_weight, columns, preferred_element_type=jnp.float32)

    pre_act = lax.map(forward_one, jnp.arange(total, dtype=jnp.int32)).reshape(features.shape)
    output = (jax.nn.silu(pre_act) * live_mask).astype(jnp.bfloat16)
    slope = (cotangent.astype(jnp.float32) * silu_slope(pre_act) * live_mask).astype(jnp.bfloat16)
    grad_lattice = build_lattice(slope, brick_x, brick_y, brick_z)
    flat_masked = masked.reshape(total, channels, voxels)
    live_flat = live_mask.reshape(total, 1, voxels)
    weight_wide = weight.astype(jnp.float32)

    def backward_one(weight_sum, brick_index):
        window = lax.dynamic_slice(grad_lattice, (zero_idx, start_x[brick_index], start_y[brick_index], start_z[brick_index]), (channels, BE + 2, BE + 2, BE + 2))
        columns = tap_windows(window, True).astype(jnp.float32)
        back_grad = jnp.einsum("okc,kov->cv", weight_wide, columns, precision=lax.Precision.HIGHEST)
        own_input = flat_masked[brick_index].astype(jnp.float32)
        weight_sum = weight_sum + jnp.einsum("kov,cv->okc", columns, own_input, precision=lax.Precision.HIGHEST)
        return weight_sum, (back_grad * live_flat[brick_index]).astype(jnp.bfloat16)

    weight_sum, x_grad = lax.scan(backward_one, jnp.zeros((channels, 27, channels), jnp.float32), jnp.arange(total, dtype=jnp.int32))
    w_grad = weight_sum / BRICKS
    return (output, x_grad.reshape(features.shape), w_grad)
```

```python
import functools

import jax
import jax.numpy as jnp
from jax import lax
from jax.experimental import pallas as pl
from jax.experimental.pallas import tpu as pltpu
from jax.sharding import PartitionSpec as P

BE = 8
PLANE = BE * BE
VOX = BE * PLANE
BF = jnp.bfloat16
F32 = jnp.float32
NT = (((1,), (1,)), ((), ()))


def call(body, outs, ins, scratch=(), flops=0, smem=()):
    specs = [
        pl.BlockSpec(memory_space=pltpu.SMEM if k in smem else pltpu.VMEM)
        for k in range(len(ins))
    ]
    moved = sum(a.size * a.dtype.itemsize for a in ins)
    moved += sum(a.size * a.dtype.itemsize for a in outs)
    return pl.pallas_call(
        body,
        out_shape=tuple(outs),
        in_specs=specs,
        out_specs=tuple(pl.BlockSpec(memory_space=pltpu.VMEM) for _ in outs),
        scratch_shapes=list(scratch),
        compiler_params=pltpu.CompilerParams(vmem_limit_bytes=48 * 1024 * 1024),
        cost_estimate=pl.CostEstimate(flops=flops, bytes_accessed=moved, transcendentals=0),
    )(*ins)


def shape(dims, dtype):
    return jax.ShapeDtypeStruct(dims, dtype)


X_ROWS = 3 * PLANE + 16
Y_XM, Y_COT = 12 * 16, 10 * BE
Y_ROWS = Y_XM + Y_COT + 16


def spot(pos_ref):
    pos = pos_ref[0]
    return pos >> 1, pos & 1


def prep_body(pos_ref, feat_ref, occ_ref, cot_ref, xm_ref, cm_ref, up_ref, down_ref):
    px, py = spot(pos_ref)
    live = occ_ref[...].astype(F32)
    channels = feat_ref.shape[0]
    xm = (feat_ref[...].astype(F32) * live).T.astype(BF)
    cm = (cot_ref[...].astype(F32) * live).T.astype(BF)
    xm_ref[...] = xm
    cm_ref[...] = cm
    at_high = jnp.full((1, channels), px, jnp.int32).astype(F32).astype(BF)
    at_low = 1 - at_high
    flag = jnp.full((16, channels), py, jnp.int32).astype(F32).astype(BF)
    up_ref[0 : 2 * PLANE] = xm[VOX - 2 * PLANE :] * at_high
    up_ref[2 * PLANE : 3 * PLANE] = cm[VOX - PLANE :] * at_high
    up_ref[3 * PLANE :] = flag
    down_ref[0 : 2 * PLANE] = xm[: 2 * PLANE] * at_low
    down_ref[2 * PLANE : 3 * PLANE] = cm[:PLANE] * at_low
    down_ref[3 * PLANE :] = flag


def weights_body(w_ref, wt_ref):
    def one(tap, carry):
        wt_ref[tap] = w_ref[tap].astype(F32).T.astype(BF)
        return carry

    lax.fori_loop(0, w_ref.shape[0], one, 0)


def x_planes(recv_ref, valid):
    channels = recv_ref.shape[1]
    xm = recv_ref[0 : 2 * PLANE].reshape(2, PLANE, channels) * valid
    cot = recv_ref[2 * PLANE : 3 * PLANE].astype(F32).reshape(1, PLANE, channels) * valid.astype(F32)
    flag = recv_ref[3 * PLANE : 3 * PLANE + 1].reshape(1, 1, channels)
    return xm, cot, (1 - flag, flag)


def scalar_rows(value, channels):
    return jnp.full((1, 1, channels), value, jnp.int32).astype(F32).astype(BF)


def strips_body(pos_ref, xm_ref, cm_ref, low_ref, high_ref, up_ref, down_ref):
    px, py = spot(pos_ref)
    channels = xm_ref.shape[1]
    one = scalar_rows(1, channels)
    own_at = (scalar_rows(1 - py, channels), scalar_rows(py, channels))
    xl, cl, at_l = x_planes(low_ref, one)
    xh, ch, at_h = x_planes(high_ref, one)
    own = xm_ref[...].reshape(BE, PLANE, channels)
    cot = cm_ref[...].astype(F32).reshape(BE, PLANE, channels)
    flag = jnp.full((16, channels), px, jnp.int32).astype(F32).astype(BF)
    for side, out in ((1, up_ref), (0, down_ref)):
        rows = slice(PLANE - 16, PLANE) if side else slice(0, 16)
        line = slice(PLANE - BE, PLANE) if side else slice(0, BE)
        out[0:32] = (xl[:, rows] * at_l[side]).reshape(32, channels)
        out[32:160] = (own[:, rows] * own_at[side]).reshape(128, channels)
        out[160:192] = (xh[:, rows] * at_h[side]).reshape(32, channels)
        lines = jnp.concatenate(
            [
                cl[:, line] * at_l[side].astype(F32),
                cot[:, line] * own_at[side].astype(F32),
                ch[:, line] * at_h[side].astype(F32),
            ],
            axis=0,
        )
        out[Y_XM : Y_XM + Y_COT] = lines.reshape(Y_COT, channels).astype(BF)
        out[Y_XM + Y_COT :] = flag


def y_rows(recv_ref, px, channels):
    strip = recv_ref[0:Y_XM].reshape(12, 16, channels)
    lines = recv_ref[Y_XM : Y_XM + Y_COT].astype(F32).reshape(10, BE, channels)
    flag = recv_ref[Y_XM + Y_COT : Y_XM + Y_COT + 1].reshape(1, 1, channels)
    zero_at, one_at = 1 - flag, flag
    here_high = scalar_rows(px, channels)
    here_low = 1 - here_high
    same = zero_at * here_low + one_at * here_high
    xm = jnp.concatenate(
        [
            strip[0:2] * here_low + strip[8:10] * (zero_at * here_high),
            strip[2:10] * same,
            strip[10:12] * here_high + strip[2:4] * (one_at * here_low),
        ],
        axis=0,
    )
    f = lambda v: v.astype(F32)
    cot = jnp.concatenate(
        [
            lines[0:1] * f(here_low) + lines[8:9] * f(zero_at * here_high),
            lines[1:9] * f(same),
            lines[9:10] * f(here_high) + lines[1:2] * f(one_at * here_low),
        ],
        axis=0,
    )
    return xm, cot


def window_body(pos_ref, xm_ref, cm_ref, xlow_ref, xhigh_ref, ylow_ref, yhigh_ref, even_ref, odd_ref, cot_ref, ring_ref):
    px, py = spot(pos_ref)
    channels = xm_ref.shape[1]
    f = lambda v: v.astype(F32)
    high_x, high_y = scalar_rows(px, channels), scalar_rows(py, channels)
    low_x, low_y = 1 - high_x, 1 - high_y
    xl, cl, at_l = x_planes(xlow_ref, low_x)
    xh, ch, at_h = x_planes(xhigh_ref, high_x)
    sl, tl = y_rows(ylow_ref, px, channels)
    sh, th = y_rows(yhigh_ref, px, channels)
    own = xm_ref[...].reshape(BE, PLANE, channels)
    cot = cm_ref[...].astype(F32).reshape(BE, PLANE, channels)
    same_l = at_l[0] * low_y + at_l[1] * high_y
    same_h = at_h[0] * low_y + at_h[1] * high_y
    none8 = jnp.zeros((BE, 16, channels), BF)
    own_low = jnp.concatenate([xl[:, 48:64] * at_l[0], none8, xh[:, 48:64] * at_h[0]], axis=0)
    own_high = jnp.concatenate([xl[:, 0:16] * at_l[1], none8, xh[:, 0:16] * at_h[1]], axis=0)
    below = sl * low_y + own_low * high_y
    above = sh * high_y + own_high * low_y
    mid = jnp.concatenate([xl * same_l, own, xh * same_h], axis=0)
    even_ref[:, 0:16] = below
    even_ref[:, 16:80] = mid
    even_ref[:, 80:96] = above
    odd = jnp.concatenate([f(below)[:, 8:16], f(mid), f(above)[:, 0:8]], axis=1).astype(BF)
    odd_ref[...] = odd
    ring = odd[1:11].reshape(800, channels)
    if channels % 128 == 64:
        cut = channels - 64
        ring_ref[0:800, :] = ring[:, :cut]
        ring_ref[800:, 0:64] = ring[0:400, cut:]
        ring_ref[800:, 64:128] = ring[400:800, cut:]
    else:
        ring_ref[...] = ring
    none8 = jnp.zeros((BE, BE, channels), F32)
    cot_low = jnp.concatenate([cl[:, 56:64] * f(at_l[0]), none8, ch[:, 56:64] * f(at_h[0])], axis=0)
    cot_high = jnp.concatenate([cl[:, 0:8] * f(at_l[1]), none8, ch[:, 0:8] * f(at_h[1])], axis=0)
    cot_below = tl * f(low_y) + cot_low * f(high_y)
    cot_above = th * f(high_y) + cot_high * f(low_y)
    cot_mid = jnp.concatenate([cl * f(same_l), cot, ch * f(same_h)], axis=0)
    cot_ref[...] = jnp.concatenate([cot_below, cot_mid, cot_above], axis=1).astype(BF)


def unpack_ring(ring):
    if ring.shape[0] == 800:
        return ring
    tail = jnp.concatenate([ring[800:, 0:64], ring[800:, 64:128]], axis=0)
    return jnp.concatenate([ring[0:800], tail], axis=1)


def z_shift(values, by):
    moved = pltpu.roll(values, by % BE, 1)
    place = lax.broadcasted_iota(jnp.int32, values.shape, 1)
    keep = place >= by if by > 0 else place < BE + by
    return jnp.where(keep, moved, 0.0)


def forward_body(parts, even_ref, odd_ref, cot_ref, occ_ref, wt_ref, out_ref, slope_ref, rows_ref):
    channels = even_ref.shape[2]
    me = lax.axis_index("gx")

    def taken(a, b):
        if b == 1:
            piece = odd_ref[a : a + 10]
        else:
            piece = even_ref[a : a + 10, 8 * b : 8 * b + 80]
        return piece.reshape(800, channels)

    pre = None
    for c in range(3):
        total = None
        for a in range(3):
            for b in range(3):
                term = jnp.dot(taken(a, b), wt_ref[9 * a + 3 * b + c], preferred_element_type=F32)
                total = term if total is None else total + term
        total = total.reshape(100, BE, channels)
        if c != 1:
            total = z_shift(total, 1 - c)
        pre = total if pre is None else pre + total
    sigma = 1.0 / (1.0 + jnp.exp(-pre))
    cot = cot_ref[...].astype(F32).reshape(100, BE, channels)
    slope = (cot * (sigma * (1.0 + pre * (1.0 - sigma)))).astype(BF)
    slope_ref[...] = slope.reshape(10, 80, channels)
    act = (pre * sigma).reshape(10, 80, channels)[1:9, 8:72].reshape(VOX, channels)
    out_ref[...] = (act.T * occ_ref[...].astype(F32)).astype(BF)
    own = slope.astype(F32).reshape(10, 80, channels)[1:9, 8:72].reshape(VOX, channels).astype(BF)
    block = channels // parts
    row = lax.broadcasted_iota(jnp.int32, (block, channels), 0)
    col = lax.broadcasted_iota(jnp.int32, (block, channels), 1)
    for k in range(parts):
        pick = (col == row + block * lax.bitwise_xor(me, jnp.int32(k))).astype(F32).astype(BF)
        rows_ref[k] = lax.dot_general(pick, own, NT, preferred_element_type=F32).astype(BF)


def backward_body(slope_ref, occ_ref, w_ref, out_ref):
    channels = slope_ref.shape[2]
    slope = slope_ref[...]
    middle = slope.astype(F32)[:, 8:72].astype(BF)
    grad = None
    for c in range(3):
        total = None
        for a in range(3):
            for b in range(3):
                if b == 1:
                    piece = middle[2 - a : 10 - a]
                else:
                    piece = slope[2 - a : 10 - a, 8 * (2 - b) : 8 * (2 - b) + 64]
                piece = piece.reshape(VOX, channels)
                term = jnp.dot(piece, w_ref[9 * a + 3 * b + c], preferred_element_type=F32)
                total = term if total is None else total + term
        total = total.reshape(PLANE, BE, channels)
        if c != 1:
            total = z_shift(total, c - 1)
        grad = total if grad is None else grad + total
    out_ref[...] = (grad.reshape(VOX, channels).T * occ_ref[...].astype(F32)).astype(BF)


def packing(width):
    full = width // 128
    rest = width - 128 * full
    per = 128 // rest if rest else 0
    return full, rest, per, 9 * full + (-(-9 // per) if rest else 0)


def lines_of(slots, rows):
    return -(-slots * rows // 16) * 16


def kernel_grad_body(parts, chips, *refs):
    rings, lines = refs[:parts], refs[parts]
    others = refs[parts + 1 : 2 * parts]
    outs = refs[2 * parts :]
    channels = 128 + (rings[0].shape[0] - 800) * 64 // 400 if rings[0].shape[0] > 800 else rings[0].shape[1]
    block = channels // parts
    width = 3 * block
    place = lax.broadcasted_iota(jnp.int32, (block, VOX), 1) & (BE - 1)
    left, windows = [], []
    for k in range(parts):
        g = (lines[0] if k == 0 else others[k - 1][...]).astype(F32)
        back = jnp.where(place < BE - 1, pltpu.roll(g, VOX - 1, 1), 0.0)
        ahead = jnp.where(place > 0, pltpu.roll(g, 1, 1), 0.0)
        left.append(jnp.concatenate([back, g, ahead], axis=0).astype(BF))
        ring = unpack_ring(rings[k][...]).reshape(10, 80, channels)
        windows.append((ring, ring.astype(F32)[:, 8:72].astype(BF)))
    left = jnp.concatenate(left, axis=1)
    full, rest, per, slots = packing(width)
    leftover = []
    store = outs[-1]
    for a in range(3):
        for b in range(3):
            right = []
            for ring, middle in windows:
                piece = middle[a : a + 8] if b == 1 else ring[a : a + 8, 8 * b : 8 * b + 64]
                right.append(piece.reshape(VOX, channels))
            total = jnp.dot(left, jnp.concatenate(right, axis=0), preferred_element_type=F32).T
            for n in range(full):
                store[(3 * a + b) * full + n] = total[:, 128 * n : 128 * n + 128]
            if rest:
                leftover.append(total[:, 128 * full :])
    if rest:
        for n in range(slots - 9 * full):
            some = leftover[n * per : (n + 1) * per]
            spare = 128 - rest * len(some)
            if spare:
                some = some + [jnp.zeros((channels, spare), F32)]
            store[9 * full + n] = jnp.concatenate(some, axis=1)
    if len(outs) == 1:
        return
    send_ref, keep_ref, _ = outs
    rows = channels // (2 * chips)
    count = lines_of(slots, rows)
    core = lax.axis_index("gy") & 1
    pad = [jnp.zeros((count - slots * rows, 128), F32)] if count > slots * rows else []
    for chip in range(chips):
        for whose, out in ((1 - core, send_ref), (core, keep_ref)):
            start = pl.multiple_of(rows * (2 * chip + whose), 8)
            piece = store[:, pl.ds(start, rows), :].reshape(slots * rows, 128)
            out[chip] = jnp.concatenate([piece] + pad, axis=0).astype(out.dtype)


def pair_body(chips, keep_ref, recv_ref, own_ref, send_ref):
    me = lax.axis_index("gy") >> 1
    own_ref[...] = keep_ref[me] + recv_ref[me].astype(F32)
    for k in range(1, chips):
        it = lax.bitwise_xor(me, jnp.int32(k))
        send_ref[k - 1] = (keep_ref[it] + recv_ref[it].astype(F32)).astype(BF)


def last_body(slots, width, scale, *refs):
    out_ref = refs[-1]
    total = refs[0][...]
    for other in refs[1:-1]:
        total = total + other[...].astype(F32)
    total = total * scale
    rows, block = out_ref.shape[1], width // 3
    full, rest, per, _ = packing(width)
    for ab in range(9):
        parts = [total[rows * (ab * full + n) : rows * (ab * full + n + 1)] for n in range(full)]
        if rest:
            at = rows * (9 * full + ab // per)
            lane = rest * (ab % per)
            parts.append(total[at : at + rows, lane : lane + rest])
        line = parts[0] if len(parts) == 1 else jnp.concatenate(parts, axis=1)
        for c in range(3):
            out_ref[3 * ab + c] = line[:, block * c : block * (c + 1)]


def xor_step(value, axis, step):
    count = lax.axis_size(axis)
    return lax.ppermute(value, axis, [(i, i ^ step) for i in range(count)])


def both_ways(up, down, axis):
    count = lax.axis_size(axis)
    forward = [(i, i + 1) for i in range(count - 1)]
    backward = [(i + 1, i) for i in range(count - 1)]
    return lax.ppermute(up, axis, forward), lax.ppermute(down, axis, backward)


def shards(features, occupancy, brick_pos, weight, cotangent):
    channels = features.shape[3]
    parts, line = lax.axis_size("gx"), lax.axis_size("gy")
    chips = line // 2
    block, rows = channels // parts, channels // line
    feat = features.reshape(channels, VOX)
    cot = cotangent.reshape(channels, VOX)
    occ = occupancy.reshape(1, VOX)
    pos = brick_pos.reshape(1)
    taps = weight.transpose(1, 0, 2)

    brick = shape((VOX, channels), BF)
    face = shape((X_ROWS, channels), BF)
    xm, cm, up, down = call(prep_body, [brick, brick, face, face], [pos, feat, occ, cot], smem=(0,))
    low, high = both_ways(up, down, "gx")
    (taps_t,) = call(weights_body, [shape(taps.shape, BF)], [taps], flops=taps.size * 64)
    strip = shape((Y_ROWS, channels), BF)
    up, down = call(strips_body, [strip, strip], [pos, xm, cm, low, high], smem=(0,))
    ylow, yhigh = both_ways(up, down, "gy")
    packed = (1200, channels - 64) if channels % 128 == 64 else (800, channels)
    even, odd, wide_cot, ring = call(
        window_body,
        [
            shape((12, 96, channels), BF),
            shape((12, 80, channels), BF),
            shape((10, 80, channels), BF),
            shape(packed, BF),
        ],
        [pos, xm, cm, low, high, ylow, yhigh],
        smem=(0,),
    )
    rings = [ring] + [xor_step(ring, "gx", k) for k in range(1, parts)]
    flops = 2 * VOX * 27 * channels * channels
    output, slope, lines = call(
        functools.partial(forward_body, parts),
        [
            shape((channels, VOX), BF),
            shape((10, 80, channels), BF),
            shape((parts, block, VOX), BF),
        ],
        [even, odd, wide_cot, occ, taps_t],
        flops=flops * 3 // 2,
    )
    others = [xor_step(lines[k], "gx", k) for k in range(1, parts)]
    (x_grad,) = call(backward_body, [shape((channels, VOX), BF)], [slope, occ, taps], flops=flops)

    width = 3 * block
    slots = packing(width)[3]
    count = lines_of(slots, rows)
    body = functools.partial(kernel_grad_body, parts, chips)
    table = (slots, channels, 128)
    if rows % 8 == 0:
        send, keep = call(
            body,
            [shape((chips, count, 128), BF), shape((chips, count, 128), F32)],
            rings + [lines] + others,
            scratch=[pltpu.VMEM(table, F32)],
            flops=flops,
        )
    else:
        (store,) = call(body, [shape(table, F32)], rings + [lines] + others, flops=flops)
        store = store.reshape(slots, chips, 2, rows, 128).transpose(2, 1, 0, 3, 4)
        store = store.reshape(2, chips, slots * rows, 128)
        store = jnp.pad(store, ((0, 0), (0, 0), (0, count - slots * rows), (0, 0)))
        core = lax.axis_index("gy") & 1
        keep = lax.dynamic_index_in_dim(store, core, 0, False)
        send = lax.dynamic_index_in_dim(store, 1 - core, 0, False).astype(BF)
    recv = xor_step(send, "gy", 1)
    own, sends = call(
        functools.partial(pair_body, chips),
        [shape((count, 128), F32), shape((chips - 1, count, 128), BF)],
        [keep, recv],
    )
    came = [xor_step(sends[k - 1], "gy", 2 * k) for k in range(1, chips)]
    (w_grad,) = call(
        functools.partial(last_body, slots, width, 1.0 / (parts * line)),
        [shape((27, rows, block), F32)],
        [own] + came,
    )
    return (
        output.reshape(features.shape),
        x_grad.reshape(features.shape),
        w_grad.transpose(2, 0, 1),
    )


def solution(mesh):
    placed = (
        P("gx", "gy", None, None, None),
        P("gx", "gy", None, None),
        P("gx", "gy", None),
        P(),
        P("gx", "gy", None, None, None),
    )
    return jax.shard_map(
        shards,
        mesh=mesh,
        in_specs=placed,
        out_specs=(
            P("gx", "gy", None, None, None),
            P("gx", "gy", None, None, None),
            P("gx", None, "gy"),
        ),
        check_vma=False,
    )
```

```python
import functools

import jax
import jax.numpy as jnp
from jax import lax
from jax.experimental import pallas as pl
from jax.experimental.pallas import tpu as pltpu
from jax.sharding import PartitionSpec as P

BE = 8
PLANE = BE * BE
VOX = BE * PLANE
BF = jnp.bfloat16
F32 = jnp.float32
NT = (((1,), (1,)), ((), ()))


def call(body, outs, ins, scratch=(), flops=0, smem=()):
    specs = [
        pl.BlockSpec(memory_space=pltpu.SMEM if k in smem else pltpu.VMEM)
        for k in range(len(ins))
    ]
    moved = sum(a.size * a.dtype.itemsize for a in ins)
    moved += sum(a.size * a.dtype.itemsize for a in outs)
    return pl.pallas_call(
        body,
        out_shape=tuple(outs),
        in_specs=specs,
        out_specs=tuple(pl.BlockSpec(memory_space=pltpu.VMEM) for _ in outs),
        scratch_shapes=list(scratch),
        compiler_params=pltpu.CompilerParams(vmem_limit_bytes=48 * 1024 * 1024),
        cost_estimate=pl.CostEstimate(flops=flops, bytes_accessed=moved, transcendentals=0),
    )(*ins)


def shape(dims, dtype):
    return jax.ShapeDtypeStruct(dims, dtype)


X_DATA = 3 * PLANE
Y_XM, Y_COT = 12 * 16, 10 * BE
Y_DATA = Y_XM + Y_COT


def packed_rows(rows, channels):
    half = -(-rows // 32) * 16 if channels % 128 == 64 else 0
    return rows + 16 + half, half


def message(rows, channels):
    if channels % 128 == 64:
        return shape((packed_rows(rows, channels)[0], channels - 64), BF)
    return shape((rows + 16, channels), BF)


def pack(out_ref, data, flag):
    rows, channels = data.shape
    _, half = packed_rows(rows, channels)
    cut = out_ref.shape[1]
    out_ref[0:rows] = data[:, :cut]
    out_ref[rows : rows + 16] = jnp.full((16, cut), flag, jnp.int32).astype(F32).astype(BF)
    if half:
        second = data[half:, cut:]
        if rows < 2 * half:
            second = jnp.concatenate([second, jnp.zeros((2 * half - rows, 64), BF)], axis=0)
        out_ref[rows + 16 :] = jnp.concatenate([data[0:half, cut:], second], axis=1)


def sides(even, odd, axis):
    place = lax.axis_index(axis) & 1
    even, odd = even[...], odd[...]
    return jnp.where(place == 1, even, odd), jnp.where(place == 1, odd, even)


def unpack(came, rows, channels):
    _, half = packed_rows(rows, channels)
    data, flag = came[0:rows], came[rows : rows + 1]
    if half:
        tail = came[rows + 16 :]
        tail = jnp.concatenate([tail[:, :64], tail[: rows - half, 64:]], axis=0)
        data = jnp.concatenate([data, tail], axis=1)
        flag = jnp.concatenate([flag, flag[:, :64]], axis=1)
    return data, flag.reshape(1, 1, channels)


def spot(pos_ref):
    pos = pos_ref[0]
    return pos >> 1, pos & 1


def prep_body(pos_ref, feat_ref, occ_ref, cot_ref, xm_ref, cm_ref, rows_ref, even_ref, odd_ref):
    px, py = spot(pos_ref)
    live = occ_ref[...].astype(F32)
    channels = feat_ref.shape[0]
    rows = feat_ref[...].astype(F32) * live
    rows_ref[...] = rows.astype(BF)
    xm = rows.T.astype(BF)
    cm = (cot_ref[...].astype(F32) * live).T.astype(BF)
    xm_ref[...] = xm
    cm_ref[...] = cm
    up = jnp.concatenate([xm[VOX - 2 * PLANE :], cm[VOX - PLANE :]], axis=0)
    down = jnp.concatenate([xm[: 2 * PLANE], cm[:PLANE]], axis=0)
    odd = lax.axis_index("gx") & 1
    for pair, out in ((0, even_ref), (1, odd_ref)):
        rises = odd == pair
        data = jnp.where(rises, up, down)
        touches = jnp.where(rises, px, 1 - px)
        data = data * jnp.full((1, channels), touches, jnp.int32).astype(F32).astype(BF)
        pack(out, data, py)


def x_planes(came, valid):
    channels = valid.shape[2]
    data, flag = unpack(came, X_DATA, channels)
    xm = data[0 : 2 * PLANE].reshape(2, PLANE, channels) * valid
    cot = data[2 * PLANE :].astype(F32).reshape(1, PLANE, channels) * valid.astype(F32)
    return xm, cot, (1 - flag, flag)


def scalar_rows(value, channels):
    return jnp.full((1, 1, channels), value, jnp.int32).astype(F32).astype(BF)


def strips_body(pos_ref, xm_ref, cm_ref, xeven_ref, xodd_ref, near_ref, even_ref, odd_ref):
    px, py = spot(pos_ref)
    channels = xm_ref.shape[1]
    one = scalar_rows(1, channels)
    own_at = (scalar_rows(1 - py, channels), scalar_rows(py, channels))
    xlow, xhigh = sides(xeven_ref, xodd_ref, "gx")
    xl, cl, at_l = x_planes(xlow, one)
    xh, ch, at_h = x_planes(xhigh, one)
    own = xm_ref[...].reshape(BE, PLANE, channels)
    cot = cm_ref[...].astype(F32).reshape(BE, PLANE, channels)
    strips = []
    for side in (0, 1):
        rows = slice(PLANE - 16, PLANE) if side else slice(0, 16)
        line = slice(PLANE - BE, PLANE) if side else slice(0, BE)
        lines = jnp.concatenate(
            [
                cl[:, line] * at_l[side].astype(F32),
                cot[:, line] * own_at[side].astype(F32),
                ch[:, line] * at_h[side].astype(F32),
            ],
            axis=0,
        )
        strip = [xl[:, rows] * at_l[side], own[:, rows] * own_at[side], xh[:, rows] * at_h[side]]
        strip = jnp.concatenate(strip, axis=0).reshape(Y_XM, channels)
        strips.append(jnp.concatenate([strip, lines.reshape(Y_COT, channels).astype(BF)], axis=0))
    place = lax.axis_index("gy") & 1
    pack(even_ref, jnp.where(place == 0, strips[1], strips[0]), px)
    pack(odd_ref, jnp.where(place == 1, strips[1], strips[0]), px)


def y_rows(came, px, channels):
    data, flag = unpack(came, Y_DATA, channels)
    strip = data[0:Y_XM].reshape(12, 16, channels)
    lines = data[Y_XM:].astype(F32).reshape(10, BE, channels)
    zero_at, one_at = 1 - flag, flag
    here_high = scalar_rows(px, channels)
    here_low = 1 - here_high
    same = zero_at * here_low + one_at * here_high
    xm = jnp.concatenate(
        [
            strip[0:2] * here_low + strip[8:10] * (zero_at * here_high),
            strip[2:10] * same,
            strip[10:12] * here_high + strip[2:4] * (one_at * here_low),
        ],
        axis=0,
    )
    f = lambda v: v.astype(F32)
    cot = jnp.concatenate(
        [
            lines[0:1] * f(here_low) + lines[8:9] * f(zero_at * here_high),
            lines[1:9] * f(same),
            lines[9:10] * f(here_high) + lines[1:2] * f(one_at * here_low),
        ],
        axis=0,
    )
    return xm, cot


def window_body(pos_ref, xm_ref, cm_ref, xeven_ref, xodd_ref, yeven_ref, yodd_ref, even_ref, odd_ref, cot_ref):
    px, py = spot(pos_ref)
    channels = xm_ref.shape[1]
    f = lambda v: v.astype(F32)
    high_x, high_y = scalar_rows(px, channels), scalar_rows(py, channels)
    low_x, low_y = 1 - high_x, 1 - high_y
    xlow, xhigh = sides(xeven_ref, xodd_ref, "gx")
    xl, cl, at_l = x_planes(xlow, low_x)
    xh, ch, at_h = x_planes(xhigh, high_x)
    ylow, yhigh = sides(yeven_ref, yodd_ref, "gy")
    sl, tl = y_rows(ylow, px, channels)
    sh, th = y_rows(yhigh, px, channels)
    own = xm_ref[...].reshape(BE, PLANE, channels)
    cot = cm_ref[...].astype(F32).reshape(BE, PLANE, channels)
    same_l = at_l[0] * low_y + at_l[1] * high_y
    same_h = at_h[0] * low_y + at_h[1] * high_y
    none8 = jnp.zeros((BE, 16, channels), BF)
    own_low = jnp.concatenate([xl[:, 48:64] * at_l[0], none8, xh[:, 48:64] * at_h[0]], axis=0)
    own_high = jnp.concatenate([xl[:, 0:16] * at_l[1], none8, xh[:, 0:16] * at_h[1]], axis=0)
    below = sl * low_y + own_low * high_y
    above = sh * high_y + own_high * low_y
    mid = jnp.concatenate([xl * same_l, own, xh * same_h], axis=0)
    even_ref[:, 0:16] = below
    even_ref[:, 16:80] = mid
    even_ref[:, 80:96] = above
    odd_ref[...] = jnp.concatenate([f(below)[:, 8:16], f(mid), f(above)[:, 0:8]], axis=1).astype(BF)
    none8 = jnp.zeros((BE, BE, channels), F32)
    cot_low = jnp.concatenate([cl[:, 56:64] * f(at_l[0]), none8, ch[:, 56:64] * f(at_h[0])], axis=0)
    cot_high = jnp.concatenate([cl[:, 0:8] * f(at_l[1]), none8, ch[:, 0:8] * f(at_h[1])], axis=0)
    cot_below = tl * f(low_y) + cot_low * f(high_y)
    cot_above = th * f(high_y) + cot_high * f(low_y)
    cot_mid = jnp.concatenate([cl * f(same_l), cot, ch * f(same_h)], axis=0)
    cot_ref[...] = jnp.concatenate([cot_below, cot_mid, cot_above], axis=1).astype(BF)


WIDE = 896


def z_shift(values, by):
    moved = pltpu.roll(values, by % BE, 1)
    place = lax.broadcasted_iota(jnp.int32, values.shape, 1)
    keep = place >= by if by > 0 else place < BE + by
    return jnp.where(keep, moved, 0.0)


def touch_body(w_ref, out_ref):
    out_ref[...] = w_ref[0, 0:16, 0:128]


def forward_body(parts, even_ref, odd_ref, cot_ref, w_ref, act_ref, slope_ref, rows_ref, wide_ref):
    channels = even_ref.shape[2]
    me = lax.axis_index("gx")
    slots = 5

    def taken(first, a, b):
        some = slice(a + first, a + first + slots)
        piece = odd_ref[some] if b == 1 else even_ref[some, 8 * b : 8 * b + 80]
        return piece.reshape(80 * slots, channels)

    for first in range(0, 10, slots):
        columns = [taken(first, a, b) for a in range(3) for b in range(3)]
        columns = jnp.concatenate(columns, axis=1)
        pre = None
        for c in range(3):
            taps = jnp.concatenate([w_ref[3 * ab + c] for ab in range(9)], axis=1)
            total = lax.dot_general(columns, taps, NT, preferred_element_type=F32)
            total = total.reshape(10 * slots, BE, channels)
            if c != 1:
                total = z_shift(total, 1 - c)
            pre = total if pre is None else pre + total
        sigma = 1.0 / (1.0 + jnp.exp(-pre))
        cot = cot_ref[first : first + slots].astype(F32).reshape(10 * slots, BE, channels)
        slope = cot * (sigma * (1.0 + pre * (1.0 - sigma)))
        slope_ref[first : first + slots] = slope.reshape(slots, 80, channels).astype(BF)
        wide_ref[first : first + slots] = (pre * sigma).reshape(slots, 80, channels)
    act_ref[...] = wide_ref[1:9, 8:72].reshape(VOX, channels).astype(BF)
    block = channels // parts
    row = lax.broadcasted_iota(jnp.int32, (channels, channels), 0)
    col = lax.broadcasted_iota(jnp.int32, (channels, channels), 1)
    wanted = jnp.zeros_like(row)
    for k in range(parts):
        start = block * lax.bitwise_xor(me, jnp.int32(k))
        wanted = jnp.where(row >= block * k, row - block * k + start, wanted)
    pick = (col == wanted).astype(F32).astype(BF)
    slope = slope_ref[...].reshape(800, channels)
    lines = lax.dot_general(pick, slope, NT, preferred_element_type=F32).astype(BF)
    for k in range(parts):
        rows_ref[k, :, 0:800] = lines[block * k : block * (k + 1)]
        rows_ref[k, :, 800:] = jnp.zeros((block, WIDE - 800), BF)


def backward_body(slope_ref, act_ref, occ_ref, w_ref, out_ref, grad_ref):
    channels = slope_ref.shape[2]
    live = occ_ref[...].astype(F32)
    out_ref[...] = (act_ref[...].astype(F32).T * live).astype(BF)
    slope = slope_ref[...]
    middle = slope.astype(F32)[:, 8:72].astype(BF)
    columns = []
    for a in range(3):
        for b in range(3):
            if b == 1:
                piece = middle[2 - a : 10 - a]
            else:
                piece = slope[2 - a : 10 - a, 8 * (2 - b) : 8 * (2 - b) + 64]
            columns.append(piece.reshape(VOX, channels))
    columns = jnp.concatenate(columns, axis=1)
    grad = None
    for c in range(3):
        taps = jnp.concatenate([w_ref[3 * ab + c] for ab in range(9)], axis=0)
        total = jnp.dot(columns, taps, preferred_element_type=F32)
        total = total.reshape(PLANE, BE, channels)
        if c != 1:
            total = z_shift(total, c - 1)
        grad = total if grad is None else grad + total
    grad_ref[...] = (grad.reshape(VOX, channels).T * live).astype(BF)


def packing(width):
    full = width // 128
    rest = width - 128 * full
    per = 128 // rest if rest else 0
    return full, rest, per, 9 * full + (-(-9 // per) if rest else 0)


def lines_of(slots, rows):
    return -(-slots * rows // 16) * 16


def kernel_grad_body(parts, chips, *refs):
    bricks, lines = refs[:parts], refs[parts]
    others = refs[parts + 1 : 2 * parts]
    outs = refs[2 * parts :]
    channels = bricks[0].shape[0]
    block = channels // parts
    width = 3 * block
    place = lax.broadcasted_iota(jnp.int32, (block, WIDE), 1) & (BE - 1)
    windows = []
    for k in range(parts):
        g = (lines[0] if k == 0 else others[k - 1][...]).astype(F32)
        back = jnp.where(place < BE - 1, pltpu.roll(g, WIDE - 1, 1), 0.0)
        ahead = jnp.where(place > 0, pltpu.roll(g, 1, 1), 0.0)
        columns = jnp.concatenate([back, g, ahead], axis=0).T[0:800].reshape(10, 80, width)
        windows.append((columns.astype(BF), columns[:, 8:72].astype(BF)))
    left = jnp.concatenate([brick[...] for brick in bricks], axis=1)
    full, rest, per, slots = packing(width)
    leftover = []
    store = outs[-1]
    for a in range(3):
        for b in range(3):
            right = []
            for window, middle in windows:
                if b == 1:
                    piece = middle[2 - a : 10 - a]
                else:
                    piece = window[2 - a : 10 - a, 8 * (2 - b) : 8 * (2 - b) + 64]
                right.append(piece.reshape(VOX, width))
            total = jnp.dot(left, jnp.concatenate(right, axis=0), preferred_element_type=F32)
            for n in range(full):
                store[(3 * a + b) * full + n] = total[:, 128 * n : 128 * n + 128]
            if rest:
                leftover.append(total[:, 128 * full :])
    if rest:
        for n in range(slots - 9 * full):
            some = leftover[n * per : (n + 1) * per]
            spare = 128 - rest * len(some)
            if spare:
                some = some + [jnp.zeros((channels, spare), F32)]
            store[9 * full + n] = jnp.concatenate(some, axis=1)
    if len(outs) == 1:
        return
    send_ref, keep_ref, _ = outs
    rows = channels // (2 * chips)
    count = lines_of(slots, rows)
    core = lax.axis_index("gy") & 1
    pad = [jnp.zeros((count - slots * rows, 128), F32)] if count > slots * rows else []
    for chip in range(chips):
        for whose, out in ((1 - core, send_ref), (core, keep_ref)):
            start = pl.multiple_of(rows * (2 * chip + whose), 8)
            piece = store[:, pl.ds(start, rows), :].reshape(slots * rows, 128)
            out[chip] = jnp.concatenate([piece] + pad, axis=0).astype(out.dtype)


def pair_body(chips, keep_ref, recv_ref, own_ref, send_ref):
    me = lax.axis_index("gy") >> 1
    own_ref[...] = keep_ref[me] + recv_ref[me].astype(F32)
    for k in range(1, chips):
        it = lax.bitwise_xor(me, jnp.int32(k))
        send_ref[k - 1] = (keep_ref[it] + recv_ref[it].astype(F32)).astype(BF)


def last_body(slots, width, scale, *refs):
    out_ref = refs[-1]
    total = refs[0][...]
    for other in refs[1:-1]:
        total = total + other[...].astype(F32)
    total = total * scale
    rows, block = out_ref.shape[1], width // 3
    full, rest, per, _ = packing(width)
    for ab in range(9):
        parts = [total[rows * (ab * full + n) : rows * (ab * full + n + 1)] for n in range(full)]
        if rest:
            at = rows * (9 * full + ab // per)
            lane = rest * (ab % per)
            parts.append(total[at : at + rows, lane : lane + rest])
        line = parts[0] if len(parts) == 1 else jnp.concatenate(parts, axis=1)
        for c in range(3):
            out_ref[3 * ab + c] = line[:, block * c : block * (c + 1)]


def xor_step(value, axis, step):
    count = lax.axis_size(axis)
    return lax.ppermute(value, axis, [(i, i ^ step) for i in range(count)])


def swap_pairs(even, odd, axis):
    count = lax.axis_size(axis)
    later = [(i, i + 1) for i in range(1, count - 1, 2)]
    odd = lax.ppermute(odd, axis, later + [(j, i) for i, j in later])
    return xor_step(even, axis, 1), odd


def shards(features, occupancy, brick_pos, weight, cotangent):
    channels = features.shape[3]
    parts, line = lax.axis_size("gx"), lax.axis_size("gy")
    chips = line // 2
    block, rows = channels // parts, channels // line
    feat = features.reshape(channels, VOX)
    cot = cotangent.reshape(channels, VOX)
    occ = occupancy.reshape(1, VOX)
    pos = brick_pos.reshape(1)
    taps = weight.transpose(1, 0, 2)

    brick, plain = shape((VOX, channels), BF), shape((channels, VOX), BF)
    face, strip = message(X_DATA, channels), message(Y_DATA, channels)
    xm, cm, masked, even, odd = call(
        prep_body,
        [brick, brick, plain, face, face],
        [pos, feat, occ, cot],
        smem=(0,),
    )
    xeven, xodd = swap_pairs(even, odd, "gx")
    bricks = {k: xor_step(masked, "gx", k) for k in reversed(range(1, parts))}
    bricks = [masked] + [bricks[k] for k in range(1, parts)]
    (near,) = call(touch_body, [shape((16, 128), BF)], [taps])
    even, odd = call(strips_body, [strip, strip], [pos, xm, cm, xeven, xodd, near], smem=(0,))
    yeven, yodd = swap_pairs(even, odd, "gy")
    even, odd, wide_cot = call(
        window_body,
        [shape((12, 96, channels), BF), shape((12, 80, channels), BF), shape((10, 80, channels), BF)],
        [pos, xm, cm, xeven, xodd, yeven, yodd],
        smem=(0,),
    )
    flops = 2 * VOX * 27 * channels * channels
    act, slope, lines = call(
        functools.partial(forward_body, parts),
        [brick, shape((10, 80, channels), BF), shape((parts, block, WIDE), BF)],
        [even, odd, wide_cot, taps],
        scratch=[pltpu.VMEM((10, 80, channels), F32)],
        flops=flops * 3 // 2,
    )
    others = {k: xor_step(lines[k], "gx", k) for k in reversed(range(1, parts))}
    others = [others[k] for k in range(1, parts)]
    output, x_grad = call(backward_body, [plain, plain], [slope, act, occ, taps], flops=flops)

    width = 3 * block
    slots = packing(width)[3]
    count = lines_of(slots, rows)
    body = functools.partial(kernel_grad_body, parts, chips)
    table = (slots, channels, 128)
    if rows % 8 == 0:
        send, keep = call(
            body,
            [shape((chips, count, 128), BF), shape((chips, count, 128), F32)],
            bricks + [lines] + others,
            scratch=[pltpu.VMEM(table, F32)],
            flops=flops,
        )
    else:
        (store,) = call(body, [shape(table, F32)], bricks + [lines] + others, flops=flops)
        store = store.reshape(slots, chips, 2, rows, 128).transpose(2, 1, 0, 3, 4)
        store = store.reshape(2, chips, slots * rows, 128)
        store = jnp.pad(store, ((0, 0), (0, 0), (0, count - slots * rows), (0, 0)))
        core = lax.axis_index("gy") & 1
        keep = lax.dynamic_index_in_dim(store, core, 0, False)
        send = lax.dynamic_index_in_dim(store, 1 - core, 0, False).astype(BF)
    recv = xor_step(send, "gy", 1)
    own, sends = call(
        functools.partial(pair_body, chips),
        [shape((count, 128), F32), shape((chips - 1, count, 128), BF)],
        [keep, recv],
    )
    came = [xor_step(sends[k - 1], "gy", 2 * k) for k in reversed(range(1, chips))]
    (w_grad,) = call(
        functools.partial(last_body, slots, width, 1.0 / (parts * line)),
        [shape((27, rows, block), F32)],
        [own] + came,
    )
    return (
        output.reshape(features.shape),
        x_grad.reshape(features.shape),
        w_grad.transpose(2, 0, 1),
    )


def solution(mesh):
    placed = (
        P("gx", "gy", None, None, None),
        P("gx", "gy", None, None),
        P("gx", "gy", None),
        P(),
        P("gx", "gy", None, None, None),
    )
    return jax.shard_map(
        shards,
        mesh=mesh,
        in_specs=placed,
        out_specs=(
            P("gx", "gy", None, None, None),
            P("gx", "gy", None, None, None),
            P("gx", None, "gy"),
        ),
        check_vma=False,
    )
```

```python
import functools

import jax
import jax.numpy as jnp
from jax import lax
from jax.experimental import pallas as pl
from jax.experimental.pallas import tpu as pltpu
from jax.sharding import PartitionSpec as P

BE = 8
PLANE = BE * BE
VOX = BE * PLANE
BF = jnp.bfloat16
F32 = jnp.float32
NT = (((1,), (1,)), ((), ()))


def call(body, outs, ins, scratch=(), flops=0, smem=(), far=(), short=False):
    space = {k: pltpu.SMEM for k in smem} | {k: pltpu.HBM for k in far}
    specs = [pl.BlockSpec(memory_space=space.get(k, pltpu.VMEM)) for k in range(len(ins))]
    ins = [
        pltpu.with_memory_space_constraint(a, pltpu.HBM) if k in far else a
        for k, a in enumerate(ins)
    ]
    moved = 0 if short else sum(a.size * a.dtype.itemsize for a in [*ins, *outs])
    return pl.pallas_call(
        body,
        out_shape=tuple(outs),
        in_specs=specs,
        out_specs=tuple(pl.BlockSpec(memory_space=pltpu.VMEM) for _ in outs),
        scratch_shapes=list(scratch),
        compiler_params=pltpu.CompilerParams(vmem_limit_bytes=48 * 1024 * 1024),
        cost_estimate=pl.CostEstimate(flops=flops, bytes_accessed=moved, transcendentals=0),
    )(*ins)


def shape(dims, dtype):
    return jax.ShapeDtypeStruct(dims, dtype)


X_DATA = 3 * PLANE
Y_XM, Y_COT = 12 * 16, 10 * BE
Y_DATA = Y_XM + Y_COT


def packed_rows(rows, channels):
    half = -(-rows // 32) * 16 if channels % 128 == 64 else 0
    return rows + 16 + half, half


def message(rows, channels):
    if channels % 128 == 64:
        return shape((packed_rows(rows, channels)[0], channels - 64), BF)
    return shape((rows + 16, channels), BF)


def pack(out_ref, data, flag):
    rows, channels = data.shape
    _, half = packed_rows(rows, channels)
    cut = out_ref.shape[1]
    out_ref[0:rows] = data[:, :cut]
    out_ref[rows : rows + 16] = jnp.full((16, cut), flag, jnp.int32).astype(F32).astype(BF)
    if half:
        second = data[half:, cut:]
        if rows < 2 * half:
            second = jnp.concatenate([second, jnp.zeros((2 * half - rows, 64), BF)], axis=0)
        out_ref[rows + 16 :] = jnp.concatenate([data[0:half, cut:], second], axis=1)


def sides(even, odd, axis):
    place = lax.axis_index(axis) & 1
    even, odd = even[...], odd[...]
    return jnp.where(place == 1, even, odd), jnp.where(place == 1, odd, even)


def unpack(came, rows, channels):
    _, half = packed_rows(rows, channels)
    data, flag = came[0:rows], came[rows : rows + 1]
    if half:
        tail = came[rows + 16 :]
        tail = jnp.concatenate([tail[:, :64], tail[: rows - half, 64:]], axis=0)
        data = jnp.concatenate([data, tail], axis=1)
        flag = jnp.concatenate([flag, flag[:, :64]], axis=1)
    return data, flag.reshape(1, 1, channels)


def spot(pos_ref):
    pos = pos_ref[0]
    return pos >> 1, pos & 1


def prep_body(pos_ref, feat_hbm, occ_hbm, cot_hbm, xm_ref, cm_ref, rows_ref, even_ref, odd_ref, feat_ref, occ_ref, cot_ref, sems):
    arrays = ((occ_hbm, occ_ref), (feat_hbm, feat_ref), (cot_hbm, cot_ref))
    copies = [pltpu.make_async_copy(a, b, sems.at[k]) for k, (a, b) in enumerate(arrays)]
    for copy in copies:
        copy.start()
    for copy in copies:
        copy.wait()
    px, py = spot(pos_ref)
    live = occ_ref[...].astype(F32)
    channels = feat_ref.shape[0]
    rows = feat_ref[...].astype(F32) * live
    rows_ref[...] = rows.astype(BF)
    xm = rows.T.astype(BF)
    cm = (cot_ref[...].astype(F32) * live).T.astype(BF)
    xm_ref[...] = xm
    cm_ref[...] = cm
    up = jnp.concatenate([xm[VOX - 2 * PLANE :], cm[VOX - PLANE :]], axis=0)
    down = jnp.concatenate([xm[: 2 * PLANE], cm[:PLANE]], axis=0)
    odd = lax.axis_index("gx") & 1
    for pair, out in ((0, even_ref), (1, odd_ref)):
        rises = odd == pair
        data = jnp.where(rises, up, down)
        touches = jnp.where(rises, px, 1 - px)
        data = data * jnp.full((1, channels), touches, jnp.int32).astype(F32).astype(BF)
        pack(out, data, py)


def x_planes(came, valid):
    channels = valid.shape[2]
    data, flag = unpack(came, X_DATA, channels)
    xm = data[0 : 2 * PLANE].reshape(2, PLANE, channels) * valid
    cot = data[2 * PLANE :].astype(F32).reshape(1, PLANE, channels) * valid.astype(F32)
    return xm, cot, (1 - flag, flag)


def scalar_rows(value, channels):
    return jnp.full((1, 1, channels), value, jnp.int32).astype(F32).astype(BF)


def strips_body(pos_ref, xm_ref, cm_ref, xeven_ref, xodd_ref, even_ref, odd_ref):
    px, py = spot(pos_ref)
    channels = xm_ref.shape[1]
    one = scalar_rows(1, channels)
    own_at = (scalar_rows(1 - py, channels), scalar_rows(py, channels))
    xlow, xhigh = sides(xeven_ref, xodd_ref, "gx")
    xl, cl, at_l = x_planes(xlow, one)
    xh, ch, at_h = x_planes(xhigh, one)
    own = xm_ref[...].reshape(BE, PLANE, channels)
    cot = cm_ref[...].astype(F32).reshape(BE, PLANE, channels)
    strips = []
    for side in (0, 1):
        rows = slice(PLANE - 16, PLANE) if side else slice(0, 16)
        line = slice(PLANE - BE, PLANE) if side else slice(0, BE)
        lines = jnp.concatenate(
            [
                cl[:, line] * at_l[side].astype(F32),
                cot[:, line] * own_at[side].astype(F32),
                ch[:, line] * at_h[side].astype(F32),
            ],
            axis=0,
        )
        strip = [xl[:, rows] * at_l[side], own[:, rows] * own_at[side], xh[:, rows] * at_h[side]]
        strip = jnp.concatenate(strip, axis=0).reshape(Y_XM, channels)
        strips.append(jnp.concatenate([strip, lines.reshape(Y_COT, channels).astype(BF)], axis=0))
    place = lax.axis_index("gy") & 1
    pack(even_ref, jnp.where(place == 0, strips[1], strips[0]), px)
    pack(odd_ref, jnp.where(place == 1, strips[1], strips[0]), px)


def y_rows(came, px, channels):
    data, flag = unpack(came, Y_DATA, channels)
    strip = data[0:Y_XM].reshape(12, 16, channels)
    lines = data[Y_XM:].astype(F32).reshape(10, BE, channels)
    zero_at, one_at = 1 - flag, flag
    here_high = scalar_rows(px, channels)
    here_low = 1 - here_high
    same = zero_at * here_low + one_at * here_high
    xm = jnp.concatenate(
        [
            strip[0:2] * here_low + strip[8:10] * (zero_at * here_high),
            strip[2:10] * same,
            strip[10:12] * here_high + strip[2:4] * (one_at * here_low),
        ],
        axis=0,
    )
    f = lambda v: v.astype(F32)
    cot = jnp.concatenate(
        [
            lines[0:1] * f(here_low) + lines[8:9] * f(zero_at * here_high),
            lines[1:9] * f(same),
            lines[9:10] * f(here_high) + lines[1:2] * f(one_at * here_low),
        ],
        axis=0,
    )
    return xm, cot


def window_body(pos_ref, xm_ref, cm_ref, xeven_ref, xodd_ref, yeven_ref, yodd_ref, near_ref, even_ref, odd_ref, cot_ref):
    px, py = spot(pos_ref)
    channels = xm_ref.shape[1]
    f = lambda v: v.astype(F32)
    high_x, high_y = scalar_rows(px, channels), scalar_rows(py, channels)
    low_x, low_y = 1 - high_x, 1 - high_y
    xlow, xhigh = sides(xeven_ref, xodd_ref, "gx")
    xl, cl, at_l = x_planes(xlow, low_x)
    xh, ch, at_h = x_planes(xhigh, high_x)
    ylow, yhigh = sides(yeven_ref, yodd_ref, "gy")
    sl, tl = y_rows(ylow, px, channels)
    sh, th = y_rows(yhigh, px, channels)
    own = xm_ref[...].reshape(BE, PLANE, channels)
    cot = cm_ref[...].astype(F32).reshape(BE, PLANE, channels)
    same_l = at_l[0] * low_y + at_l[1] * high_y
    same_h = at_h[0] * low_y + at_h[1] * high_y
    none8 = jnp.zeros((BE, 16, channels), BF)
    own_low = jnp.concatenate([xl[:, 48:64] * at_l[0], none8, xh[:, 48:64] * at_h[0]], axis=0)
    own_high = jnp.concatenate([xl[:, 0:16] * at_l[1], none8, xh[:, 0:16] * at_h[1]], axis=0)
    below = sl * low_y + own_low * high_y
    above = sh * high_y + own_high * low_y
    mid = jnp.concatenate([xl * same_l, own, xh * same_h], axis=0)
    even_ref[:, 0:16] = below
    even_ref[:, 16:80] = mid
    even_ref[:, 80:96] = above
    odd_ref[...] = jnp.concatenate([f(below)[:, 8:16], f(mid), f(above)[:, 0:8]], axis=1).astype(BF)
    none8 = jnp.zeros((BE, BE, channels), F32)
    cot_low = jnp.concatenate([cl[:, 56:64] * f(at_l[0]), none8, ch[:, 56:64] * f(at_h[0])], axis=0)
    cot_high = jnp.concatenate([cl[:, 0:8] * f(at_l[1]), none8, ch[:, 0:8] * f(at_h[1])], axis=0)
    cot_below = tl * f(low_y) + cot_low * f(high_y)
    cot_above = th * f(high_y) + cot_high * f(low_y)
    cot_mid = jnp.concatenate([cl * f(same_l), cot, ch * f(same_h)], axis=0)
    cot_ref[...] = jnp.concatenate([cot_below, cot_mid, cot_above], axis=1).astype(BF)


WIDE = 896


def z_shift(values, by):
    moved = pltpu.roll(values, by % BE, 1)
    place = lax.broadcasted_iota(jnp.int32, values.shape, 1)
    keep = place >= by if by > 0 else place < BE + by
    return jnp.where(keep, moved, 0.0)


def touch_body(w_ref, out_ref):
    out_ref[...] = w_ref[0, 0:16, 0:128]


def forward_body(parts, even_ref, odd_ref, cot_ref, w_ref, act_ref, slope_ref, rows_ref, wide_ref):
    channels = even_ref.shape[2]
    me = lax.axis_index("gx")
    slots = 5

    def taken(first, a, b):
        some = slice(a + first, a + first + slots)
        piece = odd_ref[some] if b == 1 else even_ref[some, 8 * b : 8 * b + 80]
        return piece.reshape(80 * slots, channels)

    for first in range(0, 10, slots):
        columns = [taken(first, a, b) for a in range(3) for b in range(3)]
        columns = jnp.concatenate(columns, axis=1)
        pre = None
        for c in range(3):
            taps = jnp.concatenate([w_ref[3 * ab + c] for ab in range(9)], axis=1)
            total = lax.dot_general(columns, taps, NT, preferred_element_type=F32)
            total = total.reshape(10 * slots, BE, channels)
            if c != 1:
                total = z_shift(total, 1 - c)
            pre = total if pre is None else pre + total
        sigma = 1.0 / (1.0 + jnp.exp(-pre))
        cot = cot_ref[first : first + slots].astype(F32).reshape(10 * slots, BE, channels)
        slope = cot * (sigma * (1.0 + pre * (1.0 - sigma)))
        slope_ref[first : first + slots] = slope.reshape(slots, 80, channels).astype(BF)
        wide_ref[first : first + slots] = (pre * sigma).reshape(slots, 80, channels)
    act_ref[...] = wide_ref[1:9, 8:72].reshape(VOX, channels).astype(BF)
    block = channels // parts
    row = lax.broadcasted_iota(jnp.int32, (channels, channels), 0)
    col = lax.broadcasted_iota(jnp.int32, (channels, channels), 1)
    wanted = jnp.zeros_like(row)
    for k in range(parts):
        start = block * lax.bitwise_xor(me, jnp.int32(k))
        wanted = jnp.where(row >= block * k, row - block * k + start, wanted)
    pick = (col == wanted).astype(F32).astype(BF)
    slope = slope_ref[...].reshape(800, channels)
    lines = lax.dot_general(pick, slope, NT, preferred_element_type=F32).astype(BF)
    for k in range(parts):
        rows_ref[k, :, 0:800] = lines[block * k : block * (k + 1)]
        rows_ref[k, :, 800:] = jnp.zeros((block, WIDE - 800), BF)


def backward_body(slope_ref, act_ref, occ_ref, w_ref, out_ref, grad_ref):
    channels = slope_ref.shape[2]
    live = occ_ref[...].astype(F32)
    out_ref[...] = (act_ref[...].astype(F32).T * live).astype(BF)
    slope = slope_ref[...]
    middle = slope.astype(F32)[:, 8:72].astype(BF)
    columns = []
    for a in range(3):
        for b in range(3):
            if b == 1:
                piece = middle[2 - a : 10 - a]
            else:
                piece = slope[2 - a : 10 - a, 8 * (2 - b) : 8 * (2 - b) + 64]
            columns.append(piece.reshape(VOX, channels))
    columns = jnp.concatenate(columns, axis=1)
    grad = None
    for c in range(3):
        taps = jnp.concatenate([w_ref[3 * ab + c] for ab in range(9)], axis=0)
        total = jnp.dot(columns, taps, preferred_element_type=F32)
        total = total.reshape(PLANE, BE, channels)
        if c != 1:
            total = z_shift(total, c - 1)
        grad = total if grad is None else grad + total
    grad_ref[...] = (grad.reshape(VOX, channels).T * live).astype(BF)


def packing(width):
    full = width // 128
    rest = width - 128 * full
    per = 128 // rest if rest else 0
    return full, rest, per, 9 * full + (-(-9 // per) if rest else 0)


def lines_of(slots, rows):
    return -(-slots * rows // 16) * 16


def kernel_grad_body(last, chips, *refs):
    brick_ref, line_ref = refs[:2]
    outs = refs[2:]
    before = None
    if outs[0].shape[0] == 9 and len(outs) > 1:
        before, outs = outs[0], outs[1:]
    channels = brick_ref.shape[0]
    block = line_ref.shape[0]
    width = 3 * block
    place = lax.broadcasted_iota(jnp.int32, (block, WIDE), 1) & (BE - 1)
    g = line_ref[...].astype(F32)
    back = jnp.where(place < BE - 1, pltpu.roll(g, WIDE - 1, 1), 0.0)
    ahead = jnp.where(place > 0, pltpu.roll(g, 1, 1), 0.0)
    columns = jnp.concatenate([back, g, ahead], axis=0).T[0:800].reshape(10, 80, width)
    window, middle = columns.astype(BF), columns[:, 8:72].astype(BF)
    left = brick_ref[...]
    full, rest, per, slots = packing(width)
    leftover = []
    store = outs[-1]
    for a in range(3):
        for b in range(3):
            if b == 1:
                piece = middle[2 - a : 10 - a]
            else:
                piece = window[2 - a : 10 - a, 8 * (2 - b) : 8 * (2 - b) + 64]
            total = jnp.dot(left, piece.reshape(VOX, width), preferred_element_type=F32)
            if before is not None:
                total = total + before[3 * a + b]
            if not last:
                store[3 * a + b] = total
                continue
            for n in range(full):
                store[(3 * a + b) * full + n] = total[:, 128 * n : 128 * n + 128]
            if rest:
                leftover.append(total[:, 128 * full :])
    if not last:
        return
    if rest:
        for n in range(slots - 9 * full):
            some = leftover[n * per : (n + 1) * per]
            spare = 128 - rest * len(some)
            if spare:
                some = some + [jnp.zeros((channels, spare), F32)]
            store[9 * full + n] = jnp.concatenate(some, axis=1)
    if len(outs) == 1:
        return
    send_ref, keep_ref, _ = outs
    rows = channels // (2 * chips)
    count = lines_of(slots, rows)
    core = lax.axis_index("gy") & 1
    pad = [jnp.zeros((count - slots * rows, 128), F32)] if count > slots * rows else []
    for chip in range(chips):
        for whose, out in ((1 - core, send_ref), (core, keep_ref)):
            start = pl.multiple_of(rows * (2 * chip + whose), 8)
            piece = store[:, pl.ds(start, rows), :].reshape(slots * rows, 128)
            out[chip] = jnp.concatenate([piece] + pad, axis=0).astype(out.dtype)


def pair_body(chips, keep_ref, recv_ref, own_ref, send_ref):
    me = lax.axis_index("gy") >> 1
    own_ref[...] = keep_ref[me] + recv_ref[me].astype(F32)
    for k in range(1, chips):
        it = lax.bitwise_xor(me, jnp.int32(k))
        send_ref[k - 1] = (keep_ref[it] + recv_ref[it].astype(F32)).astype(BF)


def last_body(slots, width, scale, *refs):
    out_ref = refs[-1]
    total = refs[0][...]
    for other in refs[1:-1]:
        total = total + other[...].astype(F32)
    total = total * scale
    rows, block = out_ref.shape[1], width // 3
    full, rest, per, _ = packing(width)
    for ab in range(9):
        parts = [total[rows * (ab * full + n) : rows * (ab * full + n + 1)] for n in range(full)]
        if rest:
            at = rows * (9 * full + ab // per)
            lane = rest * (ab % per)
            parts.append(total[at : at + rows, lane : lane + rest])
        line = parts[0] if len(parts) == 1 else jnp.concatenate(parts, axis=1)
        for c in range(3):
            out_ref[3 * ab + c] = line[:, block * c : block * (c + 1)]


def xor_step(value, axis, step):
    count = lax.axis_size(axis)
    return lax.ppermute(value, axis, [(i, i ^ step) for i in range(count)])


def swap_pairs(even, odd, axis):
    count = lax.axis_size(axis)
    later = [(i, i + 1) for i in range(1, count - 1, 2)]
    odd = lax.ppermute(odd, axis, later + [(j, i) for i, j in later])
    return xor_step(even, axis, 1), odd


def shards(features, occupancy, brick_pos, weight, cotangent):
    channels = features.shape[3]
    parts, line = lax.axis_size("gx"), lax.axis_size("gy")
    chips = line // 2
    block, rows = channels // parts, channels // line
    feat = features.reshape(channels, VOX)
    cot = cotangent.reshape(channels, VOX)
    occ = occupancy.reshape(1, VOX)
    pos = brick_pos.reshape(1)
    taps = weight.transpose(1, 0, 2)

    brick, plain = shape((VOX, channels), BF), shape((channels, VOX), BF)
    face, strip = message(X_DATA, channels), message(Y_DATA, channels)
    xm, cm, masked, even, odd = call(
        prep_body,
        [brick, brick, plain, face, face],
        [pos, feat, occ, cot],
        scratch=[
            pltpu.VMEM((channels, VOX), BF),
            pltpu.VMEM((1, VOX), jnp.int32),
            pltpu.VMEM((channels, VOX), BF),
            pltpu.SemaphoreType.DMA((3,)),
        ],
        smem=(0,),
        far=(1, 2, 3),
        short=True,
    )
    xeven, xodd = swap_pairs(even, odd, "gx")
    bricks = {k: xor_step(masked, "gx", k) for k in reversed(range(2, parts))}
    even, odd = call(strips_body, [strip, strip], [pos, xm, cm, xeven, xodd], smem=(0,), short=True)
    even, odd, taps, again = lax.optimization_barrier((even, odd, taps, masked))
    bricks = [masked, xor_step(again, "gx", 1)] + [bricks[k] for k in range(2, parts)]
    (near,) = call(touch_body, [shape((16, 128), BF)], [taps], flops=10**10)
    yeven, yodd = swap_pairs(even, odd, "gy")
    even, odd, wide_cot = call(
        window_body,
        [shape((12, 96, channels), BF), shape((12, 80, channels), BF), shape((10, 80, channels), BF)],
        [pos, xm, cm, xeven, xodd, yeven, yodd, near],
        smem=(0,),
        short=True,
    )
    flops = 2 * VOX * 27 * channels * channels
    act, slope, lines = call(
        functools.partial(forward_body, parts),
        [brick, shape((10, 80, channels), BF), shape((parts, block, WIDE), BF)],
        [even, odd, wide_cot, taps],
        scratch=[pltpu.VMEM((10, 80, channels), F32)],
        short=True,
    )
    others = {k: xor_step(lines[k], "gx", k) for k in reversed(range(1, parts))}
    others = [others[k] for k in range(1, parts)]
    output, x_grad = call(backward_body, [plain, plain], [slope, act, occ, taps], flops=flops)

    width = 3 * block
    slots = packing(width)[3]
    count = lines_of(slots, rows)
    table = (slots, channels, 128)
    lines = [lines[0]] + others
    so_far = []
    for k in [0, *reversed(range(2, parts))]:
        body = functools.partial(kernel_grad_body, False, chips)
        so_far = call(body, [shape((9, channels, width), F32)], [bricks[k], lines[k], *so_far], flops=flops // parts)
    body = functools.partial(kernel_grad_body, True, chips)
    ins = [bricks[1], lines[1], *so_far]
    if rows % 8 == 0:
        send, keep = call(
            body,
            [shape((chips, count, 128), BF), shape((chips, count, 128), F32)],
            ins,
            scratch=[pltpu.VMEM(table, F32)],
            flops=flops // parts,
        )
    else:
        (store,) = call(body, [shape(table, F32)], ins, flops=flops // parts)
        store = store.reshape(slots, chips, 2, rows, 128).transpose(2, 1, 0, 3, 4)
        store = store.reshape(2, chips, slots * rows, 128)
        store = jnp.pad(store, ((0, 0), (0, 0), (0, count - slots * rows), (0, 0)))
        core = lax.axis_index("gy") & 1
        keep = lax.dynamic_index_in_dim(store, core, 0, False)
        send = lax.dynamic_index_in_dim(store, 1 - core, 0, False).astype(BF)
    recv = xor_step(send, "gy", 1)
    own, sends = call(
        functools.partial(pair_body, chips),
        [shape((count, 128), F32), shape((chips - 1, count, 128), BF)],
        [keep, recv],
    )
    came = [xor_step(sends[k - 1], "gy", 2 * k) for k in range(1, chips)]
    (w_grad,) = call(
        functools.partial(last_body, slots, width, 1.0 / (parts * line)),
        [shape((27, rows, block), F32)],
        [own] + came,
    )
    return (
        output.reshape(features.shape),
        x_grad.reshape(features.shape),
        w_grad.transpose(2, 0, 1),
    )


def solution(mesh):
    placed = (
        P("gx", "gy", None, None, None),
        P("gx", "gy", None, None),
        P("gx", "gy", None),
        P(),
        P("gx", "gy", None, None, None),
    )
    return jax.shard_map(
        shards,
        mesh=mesh,
        in_specs=placed,
        out_specs=(
            P("gx", "gy", None, None, None),
            P("gx", "gy", None, None, None),
            P("gx", None, "gy"),
        ),
        check_vma=False,
    )
```

```python
import functools

import jax
import jax.numpy as jnp
from jax import lax
from jax.experimental import pallas as pl
from jax.experimental.pallas import tpu as pltpu
from jax.sharding import PartitionSpec as P

BE = 8
PLANE = BE * BE
VOX = BE * PLANE
BF = jnp.bfloat16
F32 = jnp.float32
NT = (((1,), (1,)), ((), ()))


def call(body, outs, ins, scratch=(), flops=0, far=(), anywhere=(), short=False):
    space = {k: pl.ANY for k in anywhere} | {k: pltpu.HBM for k in far}
    specs = [pl.BlockSpec(memory_space=space.get(k, pltpu.VMEM)) for k in range(len(ins))]
    ins = [
        pltpu.with_memory_space_constraint(a, pltpu.HBM) if k in far else a
        for k, a in enumerate(ins)
    ]
    moved = 0 if short else sum(a.size * a.dtype.itemsize for a in [*ins, *outs])
    return pl.pallas_call(
        body,
        out_shape=tuple(outs),
        in_specs=specs,
        out_specs=tuple(pl.BlockSpec(memory_space=pltpu.VMEM) for _ in outs),
        scratch_shapes=list(scratch),
        compiler_params=pltpu.CompilerParams(vmem_limit_bytes=48 * 1024 * 1024),
        cost_estimate=pl.CostEstimate(flops=flops, bytes_accessed=moved, transcendentals=0),
    )(*ins)


def shape(dims, dtype):
    return jax.ShapeDtypeStruct(dims, dtype)


X_DATA = 3 * PLANE
Y_XM, Y_COT = 12 * 16, 10 * BE
Y_DATA = Y_XM + Y_COT


def packed_rows(rows, channels):
    half = -(-rows // 32) * 16 if channels % 128 == 64 else 0
    return rows + 16 + half, half


def message(rows, channels):
    if channels % 128 == 64:
        return shape((packed_rows(rows, channels)[0], channels - 64), BF)
    return shape((rows + 16, channels), BF)


def pack(out_ref, data, flag):
    rows, channels = data.shape
    _, half = packed_rows(rows, channels)
    cut = out_ref.shape[1]
    out_ref[0:rows] = data[:, :cut]
    out_ref[rows : rows + 16] = flag[:, :cut] + jnp.zeros((16, cut), BF)
    if half:
        second = data[half:, cut:]
        if rows < 2 * half:
            second = jnp.concatenate([second, jnp.zeros((2 * half - rows, 64), BF)], axis=0)
        out_ref[rows + 16 :] = jnp.concatenate([data[0:half, cut:], second], axis=1)


def sides(even, odd, axis):
    place = lax.axis_index(axis) & 1
    even, odd = even[...], odd[...]
    return jnp.where(place == 1, even, odd), jnp.where(place == 1, odd, even)


def unpack(came, rows, channels):
    _, half = packed_rows(rows, channels)
    data, flag = came[0:rows], came[rows : rows + 1]
    if half:
        tail = came[rows + 16 :]
        tail = jnp.concatenate([tail[:, :64], tail[: rows - half, 64:]], axis=0)
        data = jnp.concatenate([data, tail], axis=1)
        flag = jnp.concatenate([flag, flag[:, :64]], axis=1)
    return data, flag.reshape(1, 1, channels)


def spot(spot_ref):
    return spot_ref[0:1], spot_ref[16:17]


def prep_body(
    pos_hbm, feat_hbm, occ_hbm, cot_hbm, xm_ref, cm_ref, rows_ref, even_ref, odd_ref, spot_ref, pos_ref, feat_ref, occ_ref, cot_ref, sems
):
    arrays = ((pos_hbm, pos_ref), (occ_hbm, occ_ref), (feat_hbm, feat_ref), (cot_hbm, cot_ref))
    copies = [pltpu.make_async_copy(a, b, sems.at[k]) for k, (a, b) in enumerate(arrays)]
    for copy in copies:
        copy.start()
    channels = feat_ref.shape[0]
    for copy in copies[:3]:
        copy.wait()
    pos = jnp.full((1, channels), pos_ref[0, 0, 0], jnp.int32)
    px, py = [place.astype(F32).astype(BF) for place in (pos >> 1, pos & 1)]
    spot_ref[0:16] = px + jnp.zeros((16, channels), BF)
    spot_ref[16:32] = py + jnp.zeros((16, channels), BF)
    live = occ_ref[...].astype(F32)
    rows = feat_ref[...].astype(F32) * live
    rows_ref[...] = rows.astype(BF)
    xm = rows.T.astype(BF)
    xm_ref[...] = xm
    copies[3].wait()
    cm = (cot_ref[...].astype(F32) * live).T.astype(BF)
    cm_ref[...] = cm
    up = jnp.concatenate([xm[VOX - 2 * PLANE :], cm[VOX - PLANE :]], axis=0)
    down = jnp.concatenate([xm[: 2 * PLANE], cm[:PLANE]], axis=0)
    odd = lax.axis_index("gx") & 1
    for pair, out in ((0, even_ref), (1, odd_ref)):
        rises = odd == pair
        pack(out, jnp.where(rises, up * px, down * (1 - px)), py)


def x_planes(came, valid):
    channels = valid.shape[2]
    data, flag = unpack(came, X_DATA, channels)
    xm = data[0 : 2 * PLANE].reshape(2, PLANE, channels) * valid
    cot = data[2 * PLANE :].astype(F32).reshape(1, PLANE, channels) * valid.astype(F32)
    return xm, cot, (1 - flag, flag)


def strips_body(spot_ref, xm_ref, cm_ref, xeven_ref, xodd_ref, fetched_ref, even_ref, odd_ref):
    px, py = spot(spot_ref)
    channels = xm_ref.shape[1]
    one = jnp.ones((1, 1, channels), BF)
    own_at = ((1 - py).reshape(1, 1, channels), py.reshape(1, 1, channels))
    xlow, xhigh = sides(xeven_ref, xodd_ref, "gx")
    xl, cl, at_l = x_planes(xlow, one)
    xh, ch, at_h = x_planes(xhigh, one)
    own = xm_ref[...].reshape(BE, PLANE, channels)
    cot = cm_ref[...].astype(F32).reshape(BE, PLANE, channels)
    strips = []
    for side in (0, 1):
        rows = slice(PLANE - 16, PLANE) if side else slice(0, 16)
        line = slice(PLANE - BE, PLANE) if side else slice(0, BE)
        lines = jnp.concatenate(
            [
                cl[:, line] * at_l[side].astype(F32),
                cot[:, line] * own_at[side].astype(F32),
                ch[:, line] * at_h[side].astype(F32),
            ],
            axis=0,
        )
        strip = [xl[:, rows] * at_l[side], own[:, rows] * own_at[side], xh[:, rows] * at_h[side]]
        strip = jnp.concatenate(strip, axis=0).reshape(Y_XM, channels)
        strips.append(jnp.concatenate([strip, lines.reshape(Y_COT, channels).astype(BF)], axis=0))
    place = lax.axis_index("gy") & 1
    pack(even_ref, jnp.where(place == 0, strips[1], strips[0]), px)
    pack(odd_ref, jnp.where(place == 1, strips[1], strips[0]), px)


def y_rows(came, px, channels):
    data, flag = unpack(came, Y_DATA, channels)
    strip = data[0:Y_XM].reshape(12, 16, channels)
    lines = data[Y_XM:].astype(F32).reshape(10, BE, channels)
    zero_at, one_at = 1 - flag, flag
    here_high = px.reshape(1, 1, channels)
    here_low = 1 - here_high
    same = zero_at * here_low + one_at * here_high
    xm = jnp.concatenate(
        [
            strip[0:2] * here_low + strip[8:10] * (zero_at * here_high),
            strip[2:10] * same,
            strip[10:12] * here_high + strip[2:4] * (one_at * here_low),
        ],
        axis=0,
    )
    f = lambda v: v.astype(F32)
    cot = jnp.concatenate(
        [
            lines[0:1] * f(here_low) + lines[8:9] * f(zero_at * here_high),
            lines[1:9] * f(same),
            lines[9:10] * f(here_high) + lines[1:2] * f(one_at * here_low),
        ],
        axis=0,
    )
    return xm, cot


def window_body(spot_ref, xm_ref, cm_ref, xeven_ref, xodd_ref, yeven_ref, yodd_ref, brick_ref, even_ref, odd_ref, cot_ref):
    px, py = spot(spot_ref)
    channels = xm_ref.shape[1]
    f = lambda v: v.astype(F32)
    high_x, high_y = px.reshape(1, 1, channels), py.reshape(1, 1, channels)
    low_x, low_y = 1 - high_x, 1 - high_y
    xlow, xhigh = sides(xeven_ref, xodd_ref, "gx")
    xl, cl, at_l = x_planes(xlow, low_x)
    xh, ch, at_h = x_planes(xhigh, high_x)
    ylow, yhigh = sides(yeven_ref, yodd_ref, "gy")
    sl, tl = y_rows(ylow, px, channels)
    sh, th = y_rows(yhigh, px, channels)
    own = xm_ref[...].reshape(BE, PLANE, channels)
    cot = cm_ref[...].astype(F32).reshape(BE, PLANE, channels)
    same_l = at_l[0] * low_y + at_l[1] * high_y
    same_h = at_h[0] * low_y + at_h[1] * high_y
    none8 = jnp.zeros((BE, 16, channels), BF)
    own_low = jnp.concatenate([xl[:, 48:64] * at_l[0], none8, xh[:, 48:64] * at_h[0]], axis=0)
    own_high = jnp.concatenate([xl[:, 0:16] * at_l[1], none8, xh[:, 0:16] * at_h[1]], axis=0)
    below = sl * low_y + own_low * high_y
    above = sh * high_y + own_high * low_y
    mid = jnp.concatenate([xl * same_l, own, xh * same_h], axis=0)
    even_ref[:, 0:16] = below
    even_ref[:, 16:80] = mid
    even_ref[:, 80:96] = above
    odd_ref[...] = jnp.concatenate([f(below)[:, 8:16], f(mid), f(above)[:, 0:8]], axis=1).astype(BF)
    none8 = jnp.zeros((BE, BE, channels), F32)
    cot_low = jnp.concatenate([cl[:, 56:64] * f(at_l[0]), none8, ch[:, 56:64] * f(at_h[0])], axis=0)
    cot_high = jnp.concatenate([cl[:, 0:8] * f(at_l[1]), none8, ch[:, 0:8] * f(at_h[1])], axis=0)
    cot_below = tl * f(low_y) + cot_low * f(high_y)
    cot_above = th * f(high_y) + cot_high * f(low_y)
    cot_mid = jnp.concatenate([cl * f(same_l), cot, ch * f(same_h)], axis=0)
    cot_ref[...] = jnp.concatenate([cot_below, cot_mid, cot_above], axis=1).astype(BF)


WIDE = 896


def z_shift(values, by):
    moved = pltpu.roll(values, by % BE, 1)
    place = lax.broadcasted_iota(jnp.int32, values.shape, 1)
    keep = place >= by if by > 0 else place < BE + by
    return jnp.where(keep, moved, 0.0)


def fetch_body(w_hbm, out_ref, done_ref, sem):
    copies = [
        pltpu.make_async_copy(w_hbm.at[pl.ds(9 * k, 9)], out_ref.at[pl.ds(9 * k, 9)], sem.at[k])
        for k in range(3)
    ]
    for copy in copies:
        copy.start()
    for copy in copies:
        copy.wait()
    done_ref[...] = jnp.zeros_like(done_ref)


def forward_body(parts, even_ref, odd_ref, cot_ref, w_ref, act_ref, slope_ref, rows_ref, wide_ref):
    channels = even_ref.shape[2]
    me = lax.axis_index("gx")
    slots = 5

    def taken(first, a, b):
        some = slice(a + first, a + first + slots)
        piece = odd_ref[some] if b == 1 else even_ref[some, 8 * b : 8 * b + 80]
        return piece.reshape(80 * slots, channels)

    for first in range(0, 10, slots):
        columns = [taken(first, a, b) for a in range(3) for b in range(3)]
        columns = jnp.concatenate(columns, axis=1)
        pre = None
        for c in range(3):
            taps = jnp.concatenate([w_ref[3 * ab + c] for ab in range(9)], axis=1)
            total = lax.dot_general(columns, taps, NT, preferred_element_type=F32)
            total = total.reshape(10 * slots, BE, channels)
            if c != 1:
                total = z_shift(total, 1 - c)
            pre = total if pre is None else pre + total
        sigma = 1.0 / (1.0 + jnp.exp(-pre))
        cot = cot_ref[first : first + slots].astype(F32).reshape(10 * slots, BE, channels)
        slope = cot * (sigma * (1.0 + pre * (1.0 - sigma)))
        slope_ref[first : first + slots] = slope.reshape(slots, 80, channels).astype(BF)
        wide_ref[first : first + slots] = (pre * sigma).reshape(slots, 80, channels)
    act_ref[...] = wide_ref[1:9, 8:72].reshape(VOX, channels).astype(BF)
    block = channels // parts
    row = lax.broadcasted_iota(jnp.int32, (channels, channels), 0)
    col = lax.broadcasted_iota(jnp.int32, (channels, channels), 1)
    wanted = jnp.zeros_like(row)
    for k in range(parts):
        start = block * lax.bitwise_xor(me, jnp.int32(k))
        wanted = jnp.where(row >= block * k, row - block * k + start, wanted)
    pick = (col == wanted).astype(F32).astype(BF)
    slope = slope_ref[...].reshape(800, channels)
    lines = lax.dot_general(pick, slope, NT, preferred_element_type=F32).astype(BF)
    for k in range(parts):
        rows_ref[k, :, 0:800] = lines[block * k : block * (k + 1)]
        rows_ref[k, :, 800:] = jnp.zeros((block, WIDE - 800), BF)


def backward_body(slope_ref, act_ref, occ_ref, w_ref, out_ref, grad_ref):
    channels = slope_ref.shape[2]
    live = occ_ref[...].astype(F32)
    out_ref[...] = (act_ref[...].astype(F32).T * live).astype(BF)
    slope = slope_ref[...]
    middle = slope.astype(F32)[:, 8:72].astype(BF)
    columns = []
    for a in range(3):
        for b in range(3):
            if b == 1:
                piece = middle[2 - a : 10 - a]
            else:
                piece = slope[2 - a : 10 - a, 8 * (2 - b) : 8 * (2 - b) + 64]
            columns.append(piece.reshape(VOX, channels))
    columns = jnp.concatenate(columns, axis=1)
    grad = None
    for c in range(3):
        taps = jnp.concatenate([w_ref[3 * ab + c] for ab in range(9)], axis=0)
        total = jnp.dot(columns, taps, preferred_element_type=F32)
        total = total.reshape(PLANE, BE, channels)
        if c != 1:
            total = z_shift(total, c - 1)
        grad = total if grad is None else grad + total
    grad_ref[...] = (grad.reshape(VOX, channels).T * live).astype(BF)


def packing(width):
    full = width // 128
    rest = width - 128 * full
    per = 128 // rest if rest else 0
    return full, rest, per, 9 * full + (-(-9 // per) if rest else 0)


def lines_of(slots, rows):
    return -(-slots * rows // 16) * 16


def kernel_grad_body(last, chips, *refs):
    brick_ref, line_ref = refs[:2]
    outs = refs[2:]
    before = None
    if outs[0].shape[0] == 9 and len(outs) > 1:
        before, outs = outs[0], outs[1:]
    channels = brick_ref.shape[0]
    block = line_ref.shape[0]
    width = 3 * block
    place = lax.broadcasted_iota(jnp.int32, (block, WIDE), 1) & (BE - 1)
    g = line_ref[...].astype(F32)
    back = jnp.where(place < BE - 1, pltpu.roll(g, WIDE - 1, 1), 0.0)
    ahead = jnp.where(place > 0, pltpu.roll(g, 1, 1), 0.0)
    columns = jnp.concatenate([back, g, ahead], axis=0).T[0:800].reshape(10, 80, width)
    window, middle = columns.astype(BF), columns[:, 8:72].astype(BF)
    left = brick_ref[...]
    full, rest, per, slots = packing(width)
    leftover = []
    store = outs[-1]
    for a in range(3):
        for b in range(3):
            if b == 1:
                piece = middle[2 - a : 10 - a]
            else:
                piece = window[2 - a : 10 - a, 8 * (2 - b) : 8 * (2 - b) + 64]
            total = jnp.dot(left, piece.reshape(VOX, width), preferred_element_type=F32)
            if before is not None:
                total = total + before[3 * a + b]
            if not last:
                store[3 * a + b] = total
                continue
            for n in range(full):
                store[(3 * a + b) * full + n] = total[:, 128 * n : 128 * n + 128]
            if rest:
                leftover.append(total[:, 128 * full :])
    if not last:
        return
    if rest:
        for n in range(slots - 9 * full):
            some = leftover[n * per : (n + 1) * per]
            spare = 128 - rest * len(some)
            if spare:
                some = some + [jnp.zeros((channels, spare), F32)]
            store[9 * full + n] = jnp.concatenate(some, axis=1)
    if len(outs) == 1:
        return
    send_ref, keep_ref, _ = outs
    rows = channels // (2 * chips)
    count = lines_of(slots, rows)
    core = lax.axis_index("gy") & 1
    pad = [jnp.zeros((count - slots * rows, 128), F32)] if count > slots * rows else []
    for chip in range(chips):
        for whose, out in ((1 - core, send_ref), (core, keep_ref)):
            start = pl.multiple_of(rows * (2 * chip + whose), 8)
            piece = store[:, pl.ds(start, rows), :].reshape(slots * rows, 128)
            out[chip] = jnp.concatenate([piece] + pad, axis=0).astype(out.dtype)


def pair_body(chips, keep_ref, recv_ref, own_ref, send_ref):
    me = lax.axis_index("gy") >> 1
    own_ref[...] = keep_ref[me] + recv_ref[me].astype(F32)
    for k in range(1, chips):
        it = lax.bitwise_xor(me, jnp.int32(k))
        send_ref[k - 1] = (keep_ref[it] + recv_ref[it].astype(F32)).astype(BF)


def last_body(slots, width, scale, *refs):
    out_ref = refs[-1]
    total = refs[0][...]
    for other in refs[1:-1]:
        total = total + other[...].astype(F32)
    total = total * scale
    rows, block = out_ref.shape[1], width // 3
    full, rest, per, _ = packing(width)
    for ab in range(9):
        parts = [total[rows * (ab * full + n) : rows * (ab * full + n + 1)] for n in range(full)]
        if rest:
            at = rows * (9 * full + ab // per)
            lane = rest * (ab % per)
            parts.append(total[at : at + rows, lane : lane + rest])
        line = parts[0] if len(parts) == 1 else jnp.concatenate(parts, axis=1)
        for c in range(3):
            out_ref[3 * ab + c] = line[:, block * c : block * (c + 1)]


def xor_step(value, axis, step):
    count = lax.axis_size(axis)
    return lax.ppermute(value, axis, [(i, i ^ step) for i in range(count)])


def swap_pairs(even, odd, axis):
    count = lax.axis_size(axis)
    later = [(i, i + 1) for i in range(1, count - 1, 2)]
    odd = lax.ppermute(odd, axis, later + [(j, i) for i, j in later])
    return xor_step(even, axis, 1), odd


def shards(features, occupancy, brick_pos, weight, cotangent):
    channels = features.shape[3]
    parts, line = lax.axis_size("gx"), lax.axis_size("gy")
    chips = line // 2
    block, rows = channels // parts, channels // line
    feat = features.reshape(channels, VOX)
    cot = cotangent.reshape(channels, VOX)
    occ = occupancy.reshape(1, VOX)
    taps = weight.transpose(1, 0, 2)

    brick, plain = shape((VOX, channels), BF), shape((channels, VOX), BF)
    face, strip = message(X_DATA, channels), message(Y_DATA, channels)
    xm, cm, masked, even, odd, place = call(
        prep_body,
        [brick, brick, plain, face, face, shape((32, channels), BF)],
        [brick_pos, feat, occ, cot],
        scratch=[
            pltpu.SMEM((1, 1, 1), jnp.int32),
            pltpu.VMEM((channels, VOX), BF),
            pltpu.VMEM((1, VOX), jnp.int32),
            pltpu.VMEM((channels, VOX), BF),
            pltpu.SemaphoreType.DMA((4,)),
        ],
        anywhere=(0,),
        far=(1, 2, 3),
        short=True,
    )
    xeven, xodd = swap_pairs(even, odd, "gx")
    first = parts - 1
    bricks = {0: masked, first: xor_step(masked, "gx", first)}
    taps, fetched = call(
        fetch_body,
        [shape(taps.shape, BF), shape((16, 128), BF)],
        [taps],
        scratch=[pltpu.SemaphoreType.DMA((3,))],
        flops=10**9,
        far=(0,),
    )
    even, odd = call(strips_body, [strip, strip], [place, xm, cm, xeven, xodd, fetched], short=True)
    even, odd, again = lax.optimization_barrier((even, odd, masked))
    yeven, yodd = swap_pairs(even, odd, "gy")
    for k in reversed(range(1, parts)):
        if k != first:
            bricks[k] = xor_step(again, "gx", k)
    even, odd, wide_cot = call(
        window_body,
        [shape((12, 96, channels), BF), shape((12, 80, channels), BF), shape((10, 80, channels), BF)],
        [place, xm, cm, xeven, xodd, yeven, yodd, bricks[first]],
        short=True,
    )
    flops = 2 * VOX * 27 * channels * channels
    act, slope, lines = call(
        functools.partial(forward_body, parts),
        [brick, shape((10, 80, channels), BF), shape((parts, block, WIDE), BF)],
        [even, odd, wide_cot, taps],
        scratch=[pltpu.VMEM((10, 80, channels), F32)],
        short=True,
    )
    others = {k: xor_step(lines[k], "gx", k) for k in reversed(range(1, parts))}
    others = [others[k] for k in range(1, parts)]
    output, x_grad = call(backward_body, [plain, plain], [slope, act, occ, taps], flops=flops)

    width = 3 * block
    slots = packing(width)[3]
    count = lines_of(slots, rows)
    table = (slots, channels, 128)
    lines = [lines[0]] + others
    so_far = []
    order = [0, *reversed(range(1, parts))]
    for k in order:
        last = k == order[-1]
        body = functools.partial(kernel_grad_body, last, chips)
        ins = [bricks[k], lines[k], *so_far]
        if not last:
            so_far = call(body, [shape((9, channels, width), F32)], ins, flops=flops // parts)
    if rows % 8 == 0:
        send, keep = call(
            body,
            [shape((chips, count, 128), BF), shape((chips, count, 128), F32)],
            ins,
            scratch=[pltpu.VMEM(table, F32)],
            flops=flops // parts,
        )
    else:
        (store,) = call(body, [shape(table, F32)], ins, flops=flops // parts)
        store = store.reshape(slots, chips, 2, rows, 128).transpose(2, 1, 0, 3, 4)
        store = store.reshape(2, chips, slots * rows, 128)
        store = jnp.pad(store, ((0, 0), (0, 0), (0, count - slots * rows), (0, 0)))
        core = lax.axis_index("gy") & 1
        keep = lax.dynamic_index_in_dim(store, core, 0, False)
        send = lax.dynamic_index_in_dim(store, 1 - core, 0, False).astype(BF)
    recv = xor_step(send, "gy", 1)
    own, sends = call(
        functools.partial(pair_body, chips),
        [shape((count, 128), F32), shape((chips - 1, count, 128), BF)],
        [keep, recv],
    )
    came = [xor_step(sends[k - 1], "gy", 2 * k) for k in reversed(range(1, chips))]
    (w_grad,) = call(
        functools.partial(last_body, slots, width, 1.0 / (parts * line)),
        [shape((27, rows, block), F32)],
        [own] + came,
    )
    return (
        output.reshape(features.shape),
        x_grad.reshape(features.shape),
        w_grad.transpose(2, 0, 1),
    )


def solution(mesh):
    placed = (
        P("gx", "gy", None, None, None),
        P("gx", "gy", None, None),
        P("gx", "gy", None),
        P(),
        P("gx", "gy", None, None, None),
    )
    return jax.shard_map(
        shards,
        mesh=mesh,
        in_specs=placed,
        out_specs=(
            P("gx", "gy", None, None, None),
            P("gx", "gy", None, None, None),
            P("gx", None, "gy"),
        ),
        check_vma=False,
    )
```

```python
import functools

import jax
import jax.numpy as jnp
from jax import lax
from jax.experimental import pallas as pl
from jax.experimental.pallas import tpu as pltpu
from jax.sharding import PartitionSpec as P

BE = 8
PLANE = BE * BE
VOX = BE * PLANE
BF = jnp.bfloat16
F32 = jnp.float32
NT = (((1,), (1,)), ((), ()))


def call(body, outs, ins, scratch=(), flops=0, far=(), anywhere=(), short=False):
    space = {k: pl.ANY for k in anywhere} | {k: pltpu.HBM for k in far}
    specs = [pl.BlockSpec(memory_space=space.get(k, pltpu.VMEM)) for k in range(len(ins))]
    ins = [
        pltpu.with_memory_space_constraint(a, pltpu.HBM) if k in far else a
        for k, a in enumerate(ins)
    ]
    moved = 0 if short else sum(a.size * a.dtype.itemsize for a in [*ins, *outs])
    return pl.pallas_call(
        body,
        out_shape=tuple(outs),
        in_specs=specs,
        out_specs=tuple(pl.BlockSpec(memory_space=pltpu.VMEM) for _ in outs),
        scratch_shapes=list(scratch),
        compiler_params=pltpu.CompilerParams(vmem_limit_bytes=48 * 1024 * 1024),
        cost_estimate=pl.CostEstimate(flops=flops, bytes_accessed=moved, transcendentals=0),
    )(*ins)


def shape(dims, dtype):
    return jax.ShapeDtypeStruct(dims, dtype)


X_DATA = 3 * PLANE
Y_XM, Y_COT = 12 * 16, 10 * BE
Y_DATA = Y_XM + Y_COT


def packed_rows(rows, channels):
    half = -(-rows // 32) * 16 if channels % 128 == 64 else 0
    return rows + 16 + half, half


def message(rows, channels):
    if channels % 128 == 64:
        return shape((packed_rows(rows, channels)[0], channels - 64), BF)
    return shape((rows + 16, channels), BF)


def pack(out_ref, data, flag):
    rows, channels = data.shape
    _, half = packed_rows(rows, channels)
    cut = out_ref.shape[1]
    out_ref[0:rows] = data[:, :cut]
    out_ref[rows : rows + 16] = flag[:, :cut] + jnp.zeros((16, cut), BF)
    if half:
        second = data[half:, cut:]
        if rows < 2 * half:
            second = jnp.concatenate([second, jnp.zeros((2 * half - rows, 64), BF)], axis=0)
        out_ref[rows + 16 :] = jnp.concatenate([data[0:half, cut:], second], axis=1)


def sides(even, odd, axis):
    place = lax.axis_index(axis) & 1
    even, odd = even[...], odd[...]
    return jnp.where(place == 1, even, odd), jnp.where(place == 1, odd, even)


def unpack(came, rows, channels):
    _, half = packed_rows(rows, channels)
    data, flag = came[0:rows], came[rows : rows + 1]
    if half:
        tail = came[rows + 16 :]
        tail = jnp.concatenate([tail[:, :64], tail[: rows - half, 64:]], axis=0)
        data = jnp.concatenate([data, tail], axis=1)
        flag = jnp.concatenate([flag, flag[:, :64]], axis=1)
    return data, flag.reshape(1, 1, channels)


def spot(spot_ref):
    return spot_ref[0:1], spot_ref[16:17]


def prep_body(
    pos_hbm, feat_hbm, occ_hbm, cot_hbm, xm_ref, cm_ref, rows_ref, even_ref, odd_ref, spot_ref, pos_ref, feat_ref, occ_ref, cot_ref, sems
):
    arrays = ((pos_hbm, pos_ref), (occ_hbm, occ_ref), (feat_hbm, feat_ref), (cot_hbm, cot_ref))
    copies = [pltpu.make_async_copy(a, b, sems.at[k]) for k, (a, b) in enumerate(arrays)]
    for copy in copies:
        copy.start()
    channels = feat_ref.shape[0]
    for copy in copies[:3]:
        copy.wait()
    pos = jnp.full((1, channels), pos_ref[0, 0, 0], jnp.int32)
    px, py = [place.astype(F32).astype(BF) for place in (pos >> 1, pos & 1)]
    spot_ref[0:16] = px + jnp.zeros((16, channels), BF)
    spot_ref[16:32] = py + jnp.zeros((16, channels), BF)
    live = occ_ref[...].astype(F32)
    rows = feat_ref[...].astype(F32) * live
    rows_ref[...] = rows.astype(BF)
    xm = rows.T.astype(BF)
    xm_ref[...] = xm
    copies[3].wait()
    cm = (cot_ref[...].astype(F32) * live).T.astype(BF)
    cm_ref[...] = cm
    up = jnp.concatenate([xm[VOX - 2 * PLANE :], cm[VOX - PLANE :]], axis=0)
    down = jnp.concatenate([xm[: 2 * PLANE], cm[:PLANE]], axis=0)
    odd = lax.axis_index("gx") & 1
    for pair, out in ((0, even_ref), (1, odd_ref)):
        rises = odd == pair
        pack(out, jnp.where(rises, up * px, down * (1 - px)), py)


def x_planes(came, valid):
    channels = valid.shape[2]
    data, flag = unpack(came, X_DATA, channels)
    xm = data[0 : 2 * PLANE].reshape(2, PLANE, channels) * valid
    cot = data[2 * PLANE :].astype(F32).reshape(1, PLANE, channels) * valid.astype(F32)
    return xm, cot, (1 - flag, flag)


def strips_body(spot_ref, xm_ref, cm_ref, xeven_ref, xodd_ref, fetched_ref, even_ref, odd_ref):
    px, py = spot(spot_ref)
    channels = xm_ref.shape[1]
    one = jnp.ones((1, 1, channels), BF)
    own_at = ((1 - py).reshape(1, 1, channels), py.reshape(1, 1, channels))
    xlow, xhigh = sides(xeven_ref, xodd_ref, "gx")
    xl, cl, at_l = x_planes(xlow, one)
    xh, ch, at_h = x_planes(xhigh, one)
    own = xm_ref[...].reshape(BE, PLANE, channels)
    cot = cm_ref[...].astype(F32).reshape(BE, PLANE, channels)
    strips = []
    for side in (0, 1):
        rows = slice(PLANE - 16, PLANE) if side else slice(0, 16)
        line = slice(PLANE - BE, PLANE) if side else slice(0, BE)
        lines = jnp.concatenate(
            [
                cl[:, line] * at_l[side].astype(F32),
                cot[:, line] * own_at[side].astype(F32),
                ch[:, line] * at_h[side].astype(F32),
            ],
            axis=0,
        )
        strip = [xl[:, rows] * at_l[side], own[:, rows] * own_at[side], xh[:, rows] * at_h[side]]
        strip = jnp.concatenate(strip, axis=0).reshape(Y_XM, channels)
        strips.append(jnp.concatenate([strip, lines.reshape(Y_COT, channels).astype(BF)], axis=0))
    place = lax.axis_index("gy") & 1
    pack(even_ref, jnp.where(place == 0, strips[1], strips[0]), px)
    pack(odd_ref, jnp.where(place == 1, strips[1], strips[0]), px)


def y_rows(came, px, channels):
    data, flag = unpack(came, Y_DATA, channels)
    strip = data[0:Y_XM].reshape(12, 16, channels)
    lines = data[Y_XM:].astype(F32).reshape(10, BE, channels)
    zero_at, one_at = 1 - flag, flag
    here_high = px.reshape(1, 1, channels)
    here_low = 1 - here_high
    same = zero_at * here_low + one_at * here_high
    xm = jnp.concatenate(
        [
            strip[0:2] * here_low + strip[8:10] * (zero_at * here_high),
            strip[2:10] * same,
            strip[10:12] * here_high + strip[2:4] * (one_at * here_low),
        ],
        axis=0,
    )
    f = lambda v: v.astype(F32)
    cot = jnp.concatenate(
        [
            lines[0:1] * f(here_low) + lines[8:9] * f(zero_at * here_high),
            lines[1:9] * f(same),
            lines[9:10] * f(here_high) + lines[1:2] * f(one_at * here_low),
        ],
        axis=0,
    )
    return xm, cot


def window_body(spot_ref, xm_ref, cm_ref, xeven_ref, xodd_ref, yeven_ref, yodd_ref, even_ref, odd_ref, cot_ref):
    px, py = spot(spot_ref)
    channels = xm_ref.shape[1]
    f = lambda v: v.astype(F32)
    high_x, high_y = px.reshape(1, 1, channels), py.reshape(1, 1, channels)
    low_x, low_y = 1 - high_x, 1 - high_y
    xlow, xhigh = sides(xeven_ref, xodd_ref, "gx")
    xl, cl, at_l = x_planes(xlow, low_x)
    xh, ch, at_h = x_planes(xhigh, high_x)
    ylow, yhigh = sides(yeven_ref, yodd_ref, "gy")
    sl, tl = y_rows(ylow, px, channels)
    sh, th = y_rows(yhigh, px, channels)
    own = xm_ref[...].reshape(BE, PLANE, channels)
    cot = cm_ref[...].astype(F32).reshape(BE, PLANE, channels)
    same_l = at_l[0] * low_y + at_l[1] * high_y
    same_h = at_h[0] * low_y + at_h[1] * high_y
    none8 = jnp.zeros((BE, 16, channels), BF)
    own_low = jnp.concatenate([xl[:, 48:64] * at_l[0], none8, xh[:, 48:64] * at_h[0]], axis=0)
    own_high = jnp.concatenate([xl[:, 0:16] * at_l[1], none8, xh[:, 0:16] * at_h[1]], axis=0)
    below = sl * low_y + own_low * high_y
    above = sh * high_y + own_high * low_y
    mid = jnp.concatenate([xl * same_l, own, xh * same_h], axis=0)
    even_ref[:, 0:16] = below
    even_ref[:, 16:80] = mid
    even_ref[:, 80:96] = above
    odd_ref[...] = jnp.concatenate([f(below)[:, 8:16], f(mid), f(above)[:, 0:8]], axis=1).astype(BF)
    none8 = jnp.zeros((BE, BE, channels), F32)
    cot_low = jnp.concatenate([cl[:, 56:64] * f(at_l[0]), none8, ch[:, 56:64] * f(at_h[0])], axis=0)
    cot_high = jnp.concatenate([cl[:, 0:8] * f(at_l[1]), none8, ch[:, 0:8] * f(at_h[1])], axis=0)
    cot_below = tl * f(low_y) + cot_low * f(high_y)
    cot_above = th * f(high_y) + cot_high * f(low_y)
    cot_mid = jnp.concatenate([cl * f(same_l), cot, ch * f(same_h)], axis=0)
    cot_ref[...] = jnp.concatenate([cot_below, cot_mid, cot_above], axis=1).astype(BF)


WIDE = 896


def z_shift(values, by):
    moved = pltpu.roll(values, by % BE, 1)
    place = lax.broadcasted_iota(jnp.int32, values.shape, 1)
    keep = place >= by if by > 0 else place < BE + by
    return jnp.where(keep, moved, 0.0)


def fetch_body(w_hbm, out_ref, done_ref, sem):
    copies = [
        pltpu.make_async_copy(w_hbm.at[pl.ds(9 * k, 9)], out_ref.at[pl.ds(9 * k, 9)], sem.at[k])
        for k in range(3)
    ]
    for copy in copies:
        copy.start()
    for copy in copies:
        copy.wait()
    done_ref[...] = jnp.zeros_like(done_ref)


def forward_body(parts, even_ref, odd_ref, cot_ref, w_ref, act_ref, slope_ref, *refs):
    channels = even_ref.shape[2]
    rows_refs, wide_ref = refs[:-1], refs[-1]
    me = lax.axis_index("gx")
    slots = 5

    def taken(first, a, b):
        some = slice(a + first, a + first + slots)
        piece = odd_ref[some] if b == 1 else even_ref[some, 8 * b : 8 * b + 80]
        return piece.reshape(80 * slots, channels)

    for first in range(0, 10, slots):
        columns = [taken(first, a, b) for a in range(3) for b in range(3)]
        columns = jnp.concatenate(columns, axis=1)
        pre = None
        for c in range(3):
            taps = jnp.concatenate([w_ref[3 * ab + c] for ab in range(9)], axis=1)
            total = lax.dot_general(columns, taps, NT, preferred_element_type=F32)
            total = total.reshape(10 * slots, BE, channels)
            if c != 1:
                total = z_shift(total, 1 - c)
            pre = total if pre is None else pre + total
        sigma = 1.0 / (1.0 + jnp.exp(-pre))
        cot = cot_ref[first : first + slots].astype(F32).reshape(10 * slots, BE, channels)
        slope = cot * (sigma * (1.0 + pre * (1.0 - sigma)))
        slope_ref[first : first + slots] = slope.reshape(slots, 80, channels).astype(BF)
        wide_ref[first : first + slots] = (pre * sigma).reshape(slots, 80, channels)
    act_ref[...] = wide_ref[1:9, 8:72].reshape(VOX, channels).astype(BF)
    block = channels // parts
    row = lax.broadcasted_iota(jnp.int32, (channels, channels), 0)
    col = lax.broadcasted_iota(jnp.int32, (channels, channels), 1)
    wanted = jnp.zeros_like(row)
    for k in range(parts):
        start = block * lax.bitwise_xor(me, jnp.int32(k))
        wanted = jnp.where(row >= block * k, row - block * k + start, wanted)
    pick = (col == wanted).astype(F32).astype(BF)
    slope = slope_ref[...].reshape(800, channels)
    lines = lax.dot_general(pick, slope, NT, preferred_element_type=F32).astype(BF)
    for k in range(parts):
        rows_refs[k][:, 0:800] = lines[block * k : block * (k + 1)]
        rows_refs[k][:, 800:] = jnp.zeros((block, WIDE - 800), BF)


def window_forward_body(parts, *refs):
    halo, w_ref, outs, scratch = refs[:7], refs[7], refs[9:-4], refs[-4:]
    windows, wide_ref = scratch[:3], scratch[3]
    window_body(*halo, *windows)
    forward_body(parts, *windows, w_ref, *outs, wide_ref)


def backward_body(slope_ref, act_ref, occ_ref, w_ref, out_ref, grad_ref):
    channels = slope_ref.shape[2]
    live = occ_ref[...].astype(F32)
    out_ref[...] = (act_ref[...].astype(F32).T * live).astype(BF)
    slope = slope_ref[...]
    middle = slope.astype(F32)[:, 8:72].astype(BF)
    columns = []
    for a in range(3):
        for b in range(3):
            if b == 1:
                piece = middle[2 - a : 10 - a]
            else:
                piece = slope[2 - a : 10 - a, 8 * (2 - b) : 8 * (2 - b) + 64]
            columns.append(piece.reshape(VOX, channels))
    columns = jnp.concatenate(columns, axis=1)
    grad = None
    for c in range(3):
        taps = jnp.concatenate([w_ref[3 * ab + c] for ab in range(9)], axis=0)
        total = jnp.dot(columns, taps, preferred_element_type=F32)
        total = total.reshape(PLANE, BE, channels)
        if c != 1:
            total = z_shift(total, c - 1)
        grad = total if grad is None else grad + total
    grad_ref[...] = (grad.reshape(VOX, channels).T * live).astype(BF)


def packing(width):
    full = width // 128
    rest = width - 128 * full
    per = 128 // rest if rest else 0
    return full, rest, per, 9 * full + (-(-9 // per) if rest else 0)


def lines_of(slots, rows):
    return -(-slots * rows // 16) * 16


def kernel_grad_body(last, chips, *refs):
    brick_ref, line_ref = refs[:2]
    outs = refs[2:]
    before = None
    if outs[0].shape[0] == 9 and len(outs) > 1:
        before, outs = outs[0], outs[1:]
    channels = brick_ref.shape[0]
    block = line_ref.shape[0]
    width = 3 * block
    place = lax.broadcasted_iota(jnp.int32, (block, WIDE), 1) & (BE - 1)
    g = line_ref[...].astype(F32)
    back = jnp.where(place < BE - 1, pltpu.roll(g, WIDE - 1, 1), 0.0)
    ahead = jnp.where(place > 0, pltpu.roll(g, 1, 1), 0.0)
    columns = jnp.concatenate([back, g, ahead], axis=0).astype(BF).T[0:800].reshape(10, 80, width)
    window, middle = columns, columns.astype(F32)[:, 8:72].astype(BF)
    left = brick_ref[...]
    full, rest, per, slots = packing(width)
    leftover = []
    store = outs[-1]
    for a in range(3):
        for b in range(3):
            if b == 1:
                piece = middle[2 - a : 10 - a]
            else:
                piece = window[2 - a : 10 - a, 8 * (2 - b) : 8 * (2 - b) + 64]
            total = jnp.dot(left, piece.reshape(VOX, width), preferred_element_type=F32)
            if before is not None:
                total = total + before[3 * a + b]
            if not last:
                store[3 * a + b] = total
                continue
            for n in range(full):
                store[(3 * a + b) * full + n] = total[:, 128 * n : 128 * n + 128]
            if rest:
                leftover.append(total[:, 128 * full :])
    if not last:
        return
    if rest:
        for n in range(slots - 9 * full):
            some = leftover[n * per : (n + 1) * per]
            spare = 128 - rest * len(some)
            if spare:
                some = some + [jnp.zeros((channels, spare), F32)]
            store[9 * full + n] = jnp.concatenate(some, axis=1)
    if len(outs) == 1:
        return
    send_ref, keep_ref, _ = outs
    rows = channels // (2 * chips)
    count = lines_of(slots, rows)
    core = lax.axis_index("gy") & 1
    pad = [jnp.zeros((count - slots * rows, 128), F32)] if count > slots * rows else []
    for chip in range(chips):
        for whose, out in ((1 - core, send_ref), (core, keep_ref)):
            start = pl.multiple_of(rows * (2 * chip + whose), 8)
            piece = store[:, pl.ds(start, rows), :].reshape(slots * rows, 128)
            out[chip] = jnp.concatenate([piece] + pad, axis=0).astype(out.dtype)


def pair_body(chips, keep_ref, recv_ref, own_ref, *send_refs):
    me = lax.axis_index("gy") >> 1
    own_ref[...] = keep_ref[me] + recv_ref[me].astype(F32)
    for k in range(1, chips):
        it = lax.bitwise_xor(me, jnp.int32(k))
        send_refs[k - 1][...] = (keep_ref[it] + recv_ref[it].astype(F32)).astype(BF)


def last_body(slots, width, scale, *refs):
    out_ref = refs[-1]
    total = refs[0][...]
    for other in refs[1:-1]:
        total = total + other[...].astype(F32)
    total = total * scale
    rows, block = out_ref.shape[1], width // 3
    full, rest, per, _ = packing(width)
    for ab in range(9):
        parts = [total[rows * (ab * full + n) : rows * (ab * full + n + 1)] for n in range(full)]
        if rest:
            at = rows * (9 * full + ab // per)
            lane = rest * (ab % per)
            parts.append(total[at : at + rows, lane : lane + rest])
        line = parts[0] if len(parts) == 1 else jnp.concatenate(parts, axis=1)
        for c in range(3):
            out_ref[3 * ab + c] = line[:, block * c : block * (c + 1)]


def xor_step(value, axis, step):
    count = lax.axis_size(axis)
    return lax.ppermute(value, axis, [(i, i ^ step) for i in range(count)])


def swap_pairs(even, odd, axis):
    count = lax.axis_size(axis)
    later = [(i, i + 1) for i in range(1, count - 1, 2)]
    odd = lax.ppermute(odd, axis, later + [(j, i) for i, j in later])
    return xor_step(even, axis, 1), odd


def shards(features, occupancy, brick_pos, weight, cotangent):
    channels = features.shape[3]
    parts, line = lax.axis_size("gx"), lax.axis_size("gy")
    chips = line // 2
    block, rows = channels // parts, channels // line
    feat = features.reshape(channels, VOX)
    cot = cotangent.reshape(channels, VOX)
    occ = occupancy.reshape(1, VOX)
    taps = weight.transpose(1, 0, 2)

    brick, plain = shape((VOX, channels), BF), shape((channels, VOX), BF)
    face, strip = message(X_DATA, channels), message(Y_DATA, channels)
    xm, cm, masked, even, odd, place = call(
        prep_body,
        [brick, brick, plain, face, face, shape((32, channels), BF)],
        [brick_pos, feat, occ, cot],
        scratch=[
            pltpu.SMEM((1, 1, 1), jnp.int32),
            pltpu.VMEM((channels, VOX), BF),
            pltpu.VMEM((1, VOX), jnp.int32),
            pltpu.VMEM((channels, VOX), BF),
            pltpu.SemaphoreType.DMA((4,)),
        ],
        anywhere=(0,),
        far=(1, 2, 3),
        short=True,
    )
    xeven, xodd = swap_pairs(even, odd, "gx")
    first = parts - 1
    bricks = {0: masked, first: xor_step(masked, "gx", first)}
    taps, fetched = call(
        fetch_body,
        [shape(taps.shape, BF), shape((16, 128), BF)],
        [taps],
        scratch=[pltpu.SemaphoreType.DMA((3,))],
        flops=10**9,
        far=(0,),
    )
    even, odd = call(strips_body, [strip, strip], [place, xm, cm, xeven, xodd, fetched], short=True)
    even, odd, again = lax.optimization_barrier((even, odd, masked))
    yeven, yodd = swap_pairs(even, odd, "gy")
    for k in reversed(range(1, parts)):
        if k != first:
            bricks[k] = xor_step(again, "gx", k)
    flops = 2 * VOX * 27 * channels * channels
    act, slope, *lines = call(
        functools.partial(window_forward_body, parts),
        [brick, shape((10, 80, channels), BF), *[shape((block, WIDE), BF)] * parts],
        [place, xm, cm, xeven, xodd, yeven, yodd, taps, bricks[first]],
        scratch=[
            pltpu.VMEM((12, 96, channels), BF),
            pltpu.VMEM((12, 80, channels), BF),
            pltpu.VMEM((10, 80, channels), BF),
            pltpu.VMEM((10, 80, channels), F32),
        ],
        short=True,
    )
    others = {k: xor_step(lines[k], "gx", k) for k in reversed(range(1, parts))}
    others = [others[k] for k in range(1, parts)]
    output, x_grad = call(backward_body, [plain, plain], [slope, act, occ, taps], flops=flops)

    width = 3 * block
    slots = packing(width)[3]
    count = lines_of(slots, rows)
    table = (slots, channels, 128)
    lines = [lines[0]] + others
    so_far = []
    order = [0, *reversed(range(1, parts))]
    for k in order:
        last = k == order[-1]
        body = functools.partial(kernel_grad_body, last, chips)
        ins = [bricks[k], lines[k], *so_far]
        if not last:
            so_far = call(body, [shape((9, channels, width), F32)], ins, flops=flops // parts)
    if rows % 8 == 0:
        send, keep = call(
            body,
            [shape((chips, count, 128), BF), shape((chips, count, 128), F32)],
            ins,
            scratch=[pltpu.VMEM(table, F32)],
            flops=flops // parts,
        )
    else:
        (store,) = call(body, [shape(table, F32)], ins, flops=flops // parts)
        store = store.reshape(slots, chips, 2, rows, 128).transpose(2, 1, 0, 3, 4)
        store = store.reshape(2, chips, slots * rows, 128)
        store = jnp.pad(store, ((0, 0), (0, 0), (0, count - slots * rows), (0, 0)))
        core = lax.axis_index("gy") & 1
        keep = lax.dynamic_index_in_dim(store, core, 0, False)
        send = lax.dynamic_index_in_dim(store, 1 - core, 0, False).astype(BF)
    recv = xor_step(send, "gy", 1)
    own, *sends = call(
        functools.partial(pair_body, chips),
        [shape((count, 128), F32), *[shape((count, 128), BF)] * (chips - 1)],
        [keep, recv],
    )
    came = [xor_step(sends[k - 1], "gy", 2 * k) for k in reversed(range(1, chips))]
    (w_grad,) = call(
        functools.partial(last_body, slots, width, 1.0 / (parts * line)),
        [shape((27, rows, block), F32)],
        [own] + came,
    )
    return (
        output.reshape(features.shape),
        x_grad.reshape(features.shape),
        w_grad.transpose(2, 0, 1),
    )


def solution(mesh):
    placed = (
        P("gx", "gy", None, None, None),
        P("gx", "gy", None, None),
        P("gx", "gy", None),
        P(),
        P("gx", "gy", None, None, None),
    )
    return jax.shard_map(
        shards,
        mesh=mesh,
        in_specs=placed,
        out_specs=(
            P("gx", "gy", None, None, None),
            P("gx", "gy", None, None, None),
            P("gx", None, "gy"),
        ),
        check_vma=False,
    )
```

```python
import functools

import jax
import jax.numpy as jnp
from jax import lax
from jax.experimental import pallas as pl
from jax.experimental.pallas import tpu as pltpu
from jax.sharding import PartitionSpec as P

BE = 8
PLANE = BE * BE
VOX = BE * PLANE
BF = jnp.bfloat16
F32 = jnp.float32
NT = (((1,), (1,)), ((), ()))


def call(body, outs, ins, scratch=(), flops=0, far=(), anywhere=(), short=False):
    space = {k: pl.ANY for k in anywhere} | {k: pltpu.HBM for k in far}
    specs = [pl.BlockSpec(memory_space=space.get(k, pltpu.VMEM)) for k in range(len(ins))]
    ins = [
        pltpu.with_memory_space_constraint(a, pltpu.HBM) if k in far else a
        for k, a in enumerate(ins)
    ]
    moved = 0 if short else sum(a.size * a.dtype.itemsize for a in [*ins, *outs])
    return pl.pallas_call(
        body,
        out_shape=tuple(outs),
        in_specs=specs,
        out_specs=tuple(pl.BlockSpec(memory_space=pltpu.VMEM) for _ in outs),
        scratch_shapes=list(scratch),
        compiler_params=pltpu.CompilerParams(vmem_limit_bytes=48 * 1024 * 1024),
        cost_estimate=pl.CostEstimate(flops=flops, bytes_accessed=moved, transcendentals=0),
    )(*ins)


def shape(dims, dtype):
    return jax.ShapeDtypeStruct(dims, dtype)


X_DATA = 3 * PLANE
Y_XM, Y_COT = 12 * 16, 10 * BE
Y_DATA = Y_XM + Y_COT


def packed_rows(rows, channels):
    half = -(-rows // 32) * 16 if channels % 128 == 64 else 0
    return rows + 16 + half, half


def message(rows, channels):
    if channels % 128 == 64:
        return shape((packed_rows(rows, channels)[0], channels - 64), BF)
    return shape((rows + 16, channels), BF)


def pack(out_ref, data, flag):
    rows, channels = data.shape
    _, half = packed_rows(rows, channels)
    cut = out_ref.shape[1]
    out_ref[0:rows] = data[:, :cut]
    out_ref[rows : rows + 16] = flag[:, :cut] + jnp.zeros((16, cut), BF)
    if half:
        second = data[half:, cut:]
        if rows < 2 * half:
            second = jnp.concatenate([second, jnp.zeros((2 * half - rows, 64), BF)], axis=0)
        out_ref[rows + 16 :] = jnp.concatenate([data[0:half, cut:], second], axis=1)


def sides(even, odd, axis):
    place = lax.axis_index(axis) & 1
    even, odd = even[...], odd[...]
    return jnp.where(place == 1, even, odd), jnp.where(place == 1, odd, even)


def unpack(came, rows, channels):
    _, half = packed_rows(rows, channels)
    data, flag = came[0:rows], came[rows : rows + 1]
    if half:
        tail = came[rows + 16 :]
        tail = jnp.concatenate([tail[:, :64], tail[: rows - half, 64:]], axis=0)
        data = jnp.concatenate([data, tail], axis=1)
        flag = jnp.concatenate([flag, flag[:, :64]], axis=1)
    return data, flag.reshape(1, 1, channels)


def spot(spot_ref):
    return spot_ref[0:1], spot_ref[16:17]


def prep_body(
    pos_hbm, feat_hbm, occ_hbm, cot_hbm, xm_ref, cm_ref, rows_ref, even_ref, odd_ref, spot_ref, pos_ref, feat_ref, occ_ref, cot_ref, sems
):
    arrays = ((pos_hbm, pos_ref), (occ_hbm, occ_ref), (feat_hbm, feat_ref), (cot_hbm, cot_ref))
    copies = [pltpu.make_async_copy(a, b, sems.at[k]) for k, (a, b) in enumerate(arrays)]
    for copy in copies:
        copy.start()
    channels = feat_ref.shape[0]
    for copy in copies[:3]:
        copy.wait()
    pos = jnp.full((1, channels), pos_ref[0, 0, 0], jnp.int32)
    px, py = [place.astype(F32).astype(BF) for place in (pos >> 1, pos & 1)]
    spot_ref[0:16] = px + jnp.zeros((16, channels), BF)
    spot_ref[16:32] = py + jnp.zeros((16, channels), BF)
    live = occ_ref[...].astype(F32)
    rows = feat_ref[...].astype(F32) * live
    rows_ref[...] = rows.astype(BF)
    xm = rows.T.astype(BF)
    xm_ref[...] = xm
    copies[3].wait()
    cm = (cot_ref[...].astype(F32) * live).T.astype(BF)
    cm_ref[...] = cm
    up = jnp.concatenate([xm[VOX - 2 * PLANE :], cm[VOX - PLANE :]], axis=0)
    down = jnp.concatenate([xm[: 2 * PLANE], cm[:PLANE]], axis=0)
    odd = lax.axis_index("gx") & 1
    for pair, out in ((0, even_ref), (1, odd_ref)):
        rises = odd == pair
        pack(out, jnp.where(rises, up * px, down * (1 - px)), py)


def x_planes(came, valid):
    channels = valid.shape[2]
    data, flag = unpack(came, X_DATA, channels)
    xm = data[0 : 2 * PLANE].reshape(2, PLANE, channels) * valid
    cot = data[2 * PLANE :].astype(F32).reshape(1, PLANE, channels) * valid.astype(F32)
    return xm, cot, (1 - flag, flag)


def strips_body(spot_ref, xm_ref, cm_ref, xeven_ref, xodd_ref, fetched_ref, even_ref, odd_ref):
    px, py = spot(spot_ref)
    channels = xm_ref.shape[1]
    one = jnp.ones((1, 1, channels), BF)
    own_at = ((1 - py).reshape(1, 1, channels), py.reshape(1, 1, channels))
    xlow, xhigh = sides(xeven_ref, xodd_ref, "gx")
    xl, cl, at_l = x_planes(xlow, one)
    xh, ch, at_h = x_planes(xhigh, one)
    own = xm_ref[...].reshape(BE, PLANE, channels)
    cot = cm_ref[...].astype(F32).reshape(BE, PLANE, channels)
    strips = []
    for side in (0, 1):
        rows = slice(PLANE - 16, PLANE) if side else slice(0, 16)
        line = slice(PLANE - BE, PLANE) if side else slice(0, BE)
        lines = jnp.concatenate(
            [
                cl[:, line] * at_l[side].astype(F32),
                cot[:, line] * own_at[side].astype(F32),
                ch[:, line] * at_h[side].astype(F32),
            ],
            axis=0,
        )
        strip = [xl[:, rows] * at_l[side], own[:, rows] * own_at[side], xh[:, rows] * at_h[side]]
        strip = jnp.concatenate(strip, axis=0).reshape(Y_XM, channels)
        strips.append(jnp.concatenate([strip, lines.reshape(Y_COT, channels).astype(BF)], axis=0))
    place = lax.axis_index("gy") & 1
    pack(even_ref, jnp.where(place == 0, strips[1], strips[0]), px)
    pack(odd_ref, jnp.where(place == 1, strips[1], strips[0]), px)


def y_rows(came, px, channels):
    data, flag = unpack(came, Y_DATA, channels)
    strip = data[0:Y_XM].reshape(12, 16, channels)
    lines = data[Y_XM:].astype(F32).reshape(10, BE, channels)
    zero_at, one_at = 1 - flag, flag
    here_high = px.reshape(1, 1, channels)
    here_low = 1 - here_high
    same = zero_at * here_low + one_at * here_high
    xm = jnp.concatenate(
        [
            strip[0:2] * here_low + strip[8:10] * (zero_at * here_high),
            strip[2:10] * same,
            strip[10:12] * here_high + strip[2:4] * (one_at * here_low),
        ],
        axis=0,
    )
    f = lambda v: v.astype(F32)
    cot = jnp.concatenate(
        [
            lines[0:1] * f(here_low) + lines[8:9] * f(zero_at * here_high),
            lines[1:9] * f(same),
            lines[9:10] * f(here_high) + lines[1:2] * f(one_at * here_low),
        ],
        axis=0,
    )
    return xm, cot


def window_body(spot_ref, xm_ref, cm_ref, xeven_ref, xodd_ref, yeven_ref, yodd_ref, even_ref, odd_ref, cot_ref):
    px, py = spot(spot_ref)
    channels = xm_ref.shape[1]
    f = lambda v: v.astype(F32)
    high_x, high_y = px.reshape(1, 1, channels), py.reshape(1, 1, channels)
    low_x, low_y = 1 - high_x, 1 - high_y
    xlow, xhigh = sides(xeven_ref, xodd_ref, "gx")
    xl, cl, at_l = x_planes(xlow, low_x)
    xh, ch, at_h = x_planes(xhigh, high_x)
    ylow, yhigh = sides(yeven_ref, yodd_ref, "gy")
    sl, tl = y_rows(ylow, px, channels)
    sh, th = y_rows(yhigh, px, channels)
    own = xm_ref[...].reshape(BE, PLANE, channels)
    cot = cm_ref[...].astype(F32).reshape(BE, PLANE, channels)
    same_l = at_l[0] * low_y + at_l[1] * high_y
    same_h = at_h[0] * low_y + at_h[1] * high_y
    none8 = jnp.zeros((BE, 16, channels), BF)
    own_low = jnp.concatenate([xl[:, 48:64] * at_l[0], none8, xh[:, 48:64] * at_h[0]], axis=0)
    own_high = jnp.concatenate([xl[:, 0:16] * at_l[1], none8, xh[:, 0:16] * at_h[1]], axis=0)
    below = sl * low_y + own_low * high_y
    above = sh * high_y + own_high * low_y
    mid = jnp.concatenate([xl * same_l, own, xh * same_h], axis=0)
    even_ref[:, 0:16] = below
    even_ref[:, 16:80] = mid
    even_ref[:, 80:96] = above
    odd_ref[...] = jnp.concatenate([f(below)[:, 8:16], f(mid), f(above)[:, 0:8]], axis=1).astype(BF)
    none8 = jnp.zeros((BE, BE, channels), F32)
    cot_low = jnp.concatenate([cl[:, 56:64] * f(at_l[0]), none8, ch[:, 56:64] * f(at_h[0])], axis=0)
    cot_high = jnp.concatenate([cl[:, 0:8] * f(at_l[1]), none8, ch[:, 0:8] * f(at_h[1])], axis=0)
    cot_below = tl * f(low_y) + cot_low * f(high_y)
    cot_above = th * f(high_y) + cot_high * f(low_y)
    cot_mid = jnp.concatenate([cl * f(same_l), cot, ch * f(same_h)], axis=0)
    cot_ref[...] = jnp.concatenate([cot_below, cot_mid, cot_above], axis=1).astype(BF)


WIDE = 896


def z_shift(values, by):
    moved = pltpu.roll(values, by % BE, 1)
    place = lax.broadcasted_iota(jnp.int32, values.shape, 1)
    keep = place >= by if by > 0 else place < BE + by
    return jnp.where(keep, moved, 0.0)


def fetch_body(w_hbm, out_ref, done_ref, sem):
    copies = [
        pltpu.make_async_copy(w_hbm.at[pl.ds(9 * k, 9)], out_ref.at[pl.ds(9 * k, 9)], sem.at[k])
        for k in range(3)
    ]
    for copy in copies:
        copy.start()
    for copy in copies:
        copy.wait()
    done_ref[...] = jnp.zeros_like(done_ref)


def forward_body(parts, even_ref, odd_ref, cot_ref, w_ref, act_ref, slope_ref, *refs):
    channels = even_ref.shape[2]
    rows_refs, wide_ref = refs[:-1], refs[-1]
    me = lax.axis_index("gx")
    slots = 5

    def taken(first, a, b):
        some = slice(a + first, a + first + slots)
        piece = odd_ref[some] if b == 1 else even_ref[some, 8 * b : 8 * b + 80]
        return piece.reshape(80 * slots, channels)

    for first in range(0, 10, slots):
        columns = [taken(first, a, b) for a in range(3) for b in range(3)]
        columns = jnp.concatenate(columns, axis=1)
        pre = None
        for c in range(3):
            taps = jnp.concatenate([w_ref[3 * ab + c] for ab in range(9)], axis=1)
            total = lax.dot_general(columns, taps, NT, preferred_element_type=F32)
            total = total.reshape(10 * slots, BE, channels)
            if c != 1:
                total = z_shift(total, 1 - c)
            pre = total if pre is None else pre + total
        sigma = 1.0 / (1.0 + jnp.exp(-pre))
        cot = cot_ref[first : first + slots].astype(F32).reshape(10 * slots, BE, channels)
        slope = cot * (sigma * (1.0 + pre * (1.0 - sigma)))
        slope_ref[first : first + slots] = slope.reshape(slots, 80, channels).astype(BF)
        wide_ref[first : first + slots] = (pre * sigma).reshape(slots, 80, channels)
    act_ref[...] = wide_ref[1:9, 8:72].reshape(VOX, channels).astype(BF)
    block = channels // parts
    row = lax.broadcasted_iota(jnp.int32, (channels, channels), 0)
    col = lax.broadcasted_iota(jnp.int32, (channels, channels), 1)
    wanted = jnp.zeros_like(row)
    for k in range(parts):
        start = block * lax.bitwise_xor(me, jnp.int32(k))
        wanted = jnp.where(row >= block * k, row - block * k + start, wanted)
    pick = (col == wanted).astype(F32).astype(BF)
    slope = slope_ref[...].reshape(800, channels)
    lines = lax.dot_general(pick, slope, NT, preferred_element_type=F32).astype(BF)
    for k in range(parts):
        rows_refs[k][:, 0:800] = lines[block * k : block * (k + 1)]
        rows_refs[k][:, 800:] = jnp.zeros((block, WIDE - 800), BF)


def window_forward_body(parts, *refs):
    halo, w_ref, outs, scratch = refs[:7], refs[7], refs[9:-4], refs[-4:]
    windows, wide_ref = scratch[:3], scratch[3]
    window_body(*halo, *windows)
    forward_body(parts, *windows, w_ref, *outs, wide_ref)


def backward_body(slope_ref, act_ref, occ_ref, w_ref, out_ref, grad_ref):
    channels = slope_ref.shape[2]
    live = occ_ref[...].astype(F32)
    out_ref[...] = (act_ref[...].astype(F32).T * live).astype(BF)
    slope = slope_ref[...]
    middle = slope.astype(F32)[:, 8:72].astype(BF)
    columns = []
    for a in range(3):
        for b in range(3):
            if b == 1:
                piece = middle[2 - a : 10 - a]
            else:
                piece = slope[2 - a : 10 - a, 8 * (2 - b) : 8 * (2 - b) + 64]
            columns.append(piece.reshape(VOX, channels))
    columns = jnp.concatenate(columns, axis=1)
    grad = None
    for c in range(3):
        taps = jnp.concatenate([w_ref[3 * ab + c] for ab in range(9)], axis=0)
        total = jnp.dot(columns, taps, preferred_element_type=F32)
        total = total.reshape(PLANE, BE, channels)
        if c != 1:
            total = z_shift(total, c - 1)
        grad = total if grad is None else grad + total
    grad_ref[...] = (grad.reshape(VOX, channels).T * live).astype(BF)


def packing(width):
    full = width // 128
    rest = width - 128 * full
    per = 128 // rest if rest else 0
    return full, rest, per, 9 * full + (-(-9 // per) if rest else 0)


def folds(width, rows):
    _, rest, per, _ = packing(width)
    return bool(rest) and 9 % per == 1 and rows % 8 == 0 and rows // 8 * rest <= 128


def lines_of(width, rows):
    slots = packing(width)[3]
    used = (slots - 1) * rows + 8 if folds(width, rows) else slots * rows
    return -(-used // 16) * 16


def kernel_grad_body(last, chips, *refs):
    brick_ref, line_ref = refs[:2]
    outs = refs[2:]
    before = None
    if outs[0].shape[0] == 9 and len(outs) > 1:
        before, outs = outs[0], outs[1:]
    channels = brick_ref.shape[0]
    block = line_ref.shape[0]
    width = 3 * block
    place = lax.broadcasted_iota(jnp.int32, (block, WIDE), 1) & (BE - 1)
    g = line_ref[...].astype(F32)
    back = jnp.where(place < BE - 1, pltpu.roll(g, WIDE - 1, 1), 0.0)
    ahead = jnp.where(place > 0, pltpu.roll(g, 1, 1), 0.0)
    columns = jnp.concatenate([back, g, ahead], axis=0).astype(BF).T[0:800].reshape(10, 80, width)
    window, middle = columns, columns.astype(F32)[:, 8:72].astype(BF)
    left = brick_ref[...]
    full, rest, per, slots = packing(width)
    leftover = []
    store = outs[-1]
    for a in range(3):
        for b in range(3):
            if b == 1:
                piece = middle[2 - a : 10 - a]
            else:
                piece = window[2 - a : 10 - a, 8 * (2 - b) : 8 * (2 - b) + 64]
            total = jnp.dot(left, piece.reshape(VOX, width), preferred_element_type=F32)
            if before is not None:
                total = total + before[3 * a + b]
            if not last:
                store[3 * a + b] = total
                continue
            for n in range(full):
                store[(3 * a + b) * full + n] = total[:, 128 * n : 128 * n + 128]
            if rest:
                leftover.append(total[:, 128 * full :])
    if not last:
        return
    if rest:
        for n in range(slots - 9 * full):
            some = leftover[n * per : (n + 1) * per]
            spare = 128 - rest * len(some)
            if spare:
                some = some + [jnp.zeros((channels, spare), F32)]
            store[9 * full + n] = jnp.concatenate(some, axis=1)
    if len(outs) == 1:
        return
    send_ref, keep_ref, _ = outs
    rows = channels // (2 * chips)
    count = lines_of(width, rows)
    fold = folds(width, rows)
    core = lax.axis_index("gy") & 1
    for chip in range(chips):
        for whose, out in ((1 - core, send_ref), (core, keep_ref)):
            start = pl.multiple_of(rows * (2 * chip + whose), 8)
            piece = store[:, pl.ds(start, rows), :]
            if fold:
                tail = [piece[slots - 1, n : n + 8, :rest] for n in range(0, rows, 8)]
                tail.append(jnp.zeros((8, 128 - rest * len(tail)), F32))
                pieces = [piece[: slots - 1].reshape((slots - 1) * rows, 128), jnp.concatenate(tail, axis=1)]
            else:
                pieces = [piece.reshape(slots * rows, 128)]
            used = sum(part.shape[0] for part in pieces)
            if count > used:
                pieces.append(jnp.zeros((count - used, 128), F32))
            out[chip] = jnp.concatenate(pieces, axis=0).astype(out.dtype)


def pair_body(chips, keep_ref, recv_ref, own_ref, *send_refs):
    me = lax.axis_index("gy") >> 1
    own_ref[...] = keep_ref[me] + recv_ref[me].astype(F32)
    for k in range(1, chips):
        it = lax.bitwise_xor(me, jnp.int32(k))
        send_refs[k - 1][...] = (keep_ref[it] + recv_ref[it].astype(F32)).astype(BF)


def last_body(slots, width, scale, *refs):
    out_ref = refs[-1]
    total = refs[0][...]
    for other in refs[1:-1]:
        total = total + other[...].astype(F32)
    total = total * scale
    rows, block = out_ref.shape[1], width // 3
    full, rest, per, _ = packing(width)
    for ab in range(9):
        parts = [total[rows * (ab * full + n) : rows * (ab * full + n + 1)] for n in range(full)]
        if rest:
            at = rows * (9 * full + ab // per)
            lane = rest * (ab % per)
            if ab == 8 and folds(width, rows):
                tail = [total[at : at + 8, rest * n : rest * (n + 1)] for n in range(rows // 8)]
                parts.append(jnp.concatenate(tail, axis=0))
            else:
                parts.append(total[at : at + rows, lane : lane + rest])
        line = parts[0] if len(parts) == 1 else jnp.concatenate(parts, axis=1)
        for c in range(3):
            out_ref[3 * ab + c] = line[:, block * c : block * (c + 1)]


def xor_step(value, axis, step):
    count = lax.axis_size(axis)
    return lax.ppermute(value, axis, [(i, i ^ step) for i in range(count)])


def swap_pairs(even, odd, axis):
    count = lax.axis_size(axis)
    later = [(i, i + 1) for i in range(1, count - 1, 2)]
    odd = lax.ppermute(odd, axis, later + [(j, i) for i, j in later])
    return xor_step(even, axis, 1), odd


def shards(features, occupancy, brick_pos, weight, cotangent):
    channels = features.shape[3]
    parts, line = lax.axis_size("gx"), lax.axis_size("gy")
    chips = line // 2
    block, rows = channels // parts, channels // line
    feat = features.reshape(channels, VOX)
    cot = cotangent.reshape(channels, VOX)
    occ = occupancy.reshape(1, VOX)
    taps = weight.transpose(1, 0, 2)

    brick, plain = shape((VOX, channels), BF), shape((channels, VOX), BF)
    face, strip = message(X_DATA, channels), message(Y_DATA, channels)
    xm, cm, masked, even, odd, place = call(
        prep_body,
        [brick, brick, plain, face, face, shape((32, channels), BF)],
        [brick_pos, feat, occ, cot],
        scratch=[
            pltpu.SMEM((1, 1, 1), jnp.int32),
            pltpu.VMEM((channels, VOX), BF),
            pltpu.VMEM((1, VOX), jnp.int32),
            pltpu.VMEM((channels, VOX), BF),
            pltpu.SemaphoreType.DMA((4,)),
        ],
        anywhere=(0,),
        far=(1, 2, 3),
        short=True,
    )
    xeven, xodd = swap_pairs(even, odd, "gx")
    first = parts - 1
    bricks = {0: masked, first: xor_step(masked, "gx", first)}
    taps, fetched = call(
        fetch_body,
        [shape(taps.shape, BF), shape((16, 128), BF)],
        [taps],
        scratch=[pltpu.SemaphoreType.DMA((3,))],
        flops=10**9,
        far=(0,),
    )
    even, odd = call(strips_body, [strip, strip], [place, xm, cm, xeven, xodd, fetched], short=True)
    even, odd, again = lax.optimization_barrier((even, odd, masked))
    yeven, yodd = swap_pairs(even, odd, "gy")
    for k in reversed(range(1, parts)):
        if k != first:
            bricks[k] = xor_step(again, "gx", k)
    flops = 2 * VOX * 27 * channels * channels
    act, slope, *lines = call(
        functools.partial(window_forward_body, parts),
        [brick, shape((10, 80, channels), BF), *[shape((block, WIDE), BF)] * parts],
        [place, xm, cm, xeven, xodd, yeven, yodd, taps, bricks[first]],
        scratch=[
            pltpu.VMEM((12, 96, channels), BF),
            pltpu.VMEM((12, 80, channels), BF),
            pltpu.VMEM((10, 80, channels), BF),
            pltpu.VMEM((10, 80, channels), F32),
        ],
        short=True,
    )
    others = {k: xor_step(lines[k], "gx", k) for k in reversed(range(1, parts))}
    others = [others[k] for k in range(1, parts)]
    output, x_grad = call(backward_body, [plain, plain], [slope, act, occ, taps], flops=flops)

    width = 3 * block
    slots = packing(width)[3]
    count = lines_of(width, rows)
    table = (slots, channels, 128)
    lines = [lines[0]] + others
    so_far = []
    order = [0, *reversed(range(1, parts))]
    for k in order:
        last = k == order[-1]
        body = functools.partial(kernel_grad_body, last, chips)
        ins = [bricks[k], lines[k], *so_far]
        if not last:
            so_far = call(body, [shape((9, channels, width), F32)], ins, flops=flops // parts)
    if rows % 8 == 0:
        send, keep = call(
            body,
            [shape((chips, count, 128), BF), shape((chips, count, 128), F32)],
            ins,
            scratch=[pltpu.VMEM(table, F32)],
            flops=flops // parts,
        )
    else:
        (store,) = call(body, [shape(table, F32)], ins, flops=flops // parts)
        store = store.reshape(slots, chips, 2, rows, 128).transpose(2, 1, 0, 3, 4)
        store = store.reshape(2, chips, slots * rows, 128)
        store = jnp.pad(store, ((0, 0), (0, 0), (0, count - slots * rows), (0, 0)))
        core = lax.axis_index("gy") & 1
        keep = lax.dynamic_index_in_dim(store, core, 0, False)
        send = lax.dynamic_index_in_dim(store, 1 - core, 0, False).astype(BF)
    recv = xor_step(send, "gy", 1)
    own, *sends = call(
        functools.partial(pair_body, chips),
        [shape((count, 128), F32), *[shape((count, 128), BF)] * (chips - 1)],
        [keep, recv],
    )
    came = [xor_step(sends[k - 1], "gy", 2 * k) for k in reversed(range(1, chips))]
    (w_grad,) = call(
        functools.partial(last_body, slots, width, 1.0 / (parts * line)),
        [shape((27, rows, block), F32)],
        [own] + came,
    )
    return (
        output.reshape(features.shape),
        x_grad.reshape(features.shape),
        w_grad.transpose(2, 0, 1),
    )


def solution(mesh):
    placed = (
        P("gx", "gy", None, None, None),
        P("gx", "gy", None, None),
        P("gx", "gy", None),
        P(),
        P("gx", "gy", None, None, None),
    )
    return jax.shard_map(
        shards,
        mesh=mesh,
        in_specs=placed,
        out_specs=(
            P("gx", "gy", None, None, None),
            P("gx", "gy", None, None, None),
            P("gx", None, "gy"),
        ),
        check_vma=False,
    )
```

```python
import functools

import jax
import jax.numpy as jnp
from jax import lax
from jax.experimental import pallas as pl
from jax.experimental.pallas import tpu as pltpu
from jax.sharding import PartitionSpec as P

BE = 8
PLANE = BE * BE
VOX = BE * PLANE
BF = jnp.bfloat16
F32 = jnp.float32
NT = (((1,), (1,)), ((), ()))


def call(body, outs, ins, scratch=(), flops=0, far=(), anywhere=(), out_space=pltpu.VMEM, short=False):
    space = {k: pl.ANY for k in anywhere} | {k: pltpu.HBM for k in far}
    specs = [pl.BlockSpec(memory_space=space.get(k, pltpu.VMEM)) for k in range(len(ins))]
    ins = [
        pltpu.with_memory_space_constraint(a, pltpu.HBM) if k in far else a
        for k, a in enumerate(ins)
    ]
    moved = 0 if short else sum(a.size * a.dtype.itemsize for a in [*ins, *outs])
    return pl.pallas_call(
        body,
        out_shape=tuple(outs),
        in_specs=specs,
        out_specs=tuple(pl.BlockSpec(memory_space=out_space) for _ in outs),
        scratch_shapes=list(scratch),
        compiler_params=pltpu.CompilerParams(vmem_limit_bytes=48 * 1024 * 1024),
        cost_estimate=pl.CostEstimate(flops=flops, bytes_accessed=moved, transcendentals=0),
    )(*ins)


def shape(dims, dtype):
    return jax.ShapeDtypeStruct(dims, dtype)


X_DATA = 3 * PLANE
Y_XM, Y_COT = 12 * 16, 10 * BE
Y_DATA = Y_XM + Y_COT


def packed_rows(rows, channels):
    half = -(-rows // 32) * 16 if channels % 128 == 64 else 0
    return rows + 16 + half, half


def message(rows, channels):
    if channels % 128 == 64:
        return shape((packed_rows(rows, channels)[0], channels - 64), BF)
    return shape((rows + 16, channels), BF)


def pack(out_ref, data, flag):
    rows, channels = data.shape
    _, half = packed_rows(rows, channels)
    cut = out_ref.shape[1]
    out_ref[0:rows] = data[:, :cut]
    out_ref[rows : rows + 16] = flag[:, :cut] + jnp.zeros((16, cut), BF)
    if half:
        second = data[half:, cut:]
        if rows < 2 * half:
            second = jnp.concatenate([second, jnp.zeros((2 * half - rows, 64), BF)], axis=0)
        out_ref[rows + 16 :] = jnp.concatenate([data[0:half, cut:], second], axis=1)


def sides(even, odd, axis):
    place = lax.axis_index(axis) & 1
    even, odd = even[...], odd[...]
    return jnp.where(place == 1, even, odd), jnp.where(place == 1, odd, even)


def unpack(came, rows, channels):
    _, half = packed_rows(rows, channels)
    data, flag = came[0:rows], came[rows : rows + 1]
    if half:
        tail = came[rows + 16 :]
        tail = jnp.concatenate([tail[:, :64], tail[: rows - half, 64:]], axis=0)
        data = jnp.concatenate([data, tail], axis=1)
        flag = jnp.concatenate([flag, flag[:, :64]], axis=1)
    return data, flag.reshape(1, 1, channels)


def spot(spot_ref):
    return spot_ref[0:1], spot_ref[16:17]


def prep_body(
    pos_hbm, feat_hbm, occ_hbm, cot_hbm, xm_ref, cm_ref, rows_ref, even_ref, odd_ref, spot_ref, pos_ref, feat_ref, occ_ref, cot_ref, sems
):
    arrays = ((pos_hbm, pos_ref), (occ_hbm, occ_ref), (feat_hbm, feat_ref), (cot_hbm, cot_ref))
    copies = [pltpu.make_async_copy(a, b, sems.at[k]) for k, (a, b) in enumerate(arrays)]
    for copy in copies:
        copy.start()
    channels = feat_ref.shape[0]
    for copy in copies[:3]:
        copy.wait()
    pos = jnp.full((1, channels), pos_ref[0, 0, 0], jnp.int32)
    px, py = [place.astype(F32).astype(BF) for place in (pos >> 1, pos & 1)]
    spot_ref[0:16] = px + jnp.zeros((16, channels), BF)
    spot_ref[16:32] = py + jnp.zeros((16, channels), BF)
    live = occ_ref[...].astype(F32)
    rows = feat_ref[...].astype(F32) * live
    rows_ref[...] = rows.astype(BF)
    xm = rows.T.astype(BF)
    xm_ref[...] = xm
    copies[3].wait()
    cm = (cot_ref[...].astype(F32) * live).T.astype(BF)
    cm_ref[...] = cm
    up = jnp.concatenate([xm[VOX - 2 * PLANE :], cm[VOX - PLANE :]], axis=0)
    down = jnp.concatenate([xm[: 2 * PLANE], cm[:PLANE]], axis=0)
    odd = lax.axis_index("gx") & 1
    for pair, out in ((0, even_ref), (1, odd_ref)):
        rises = odd == pair
        pack(out, jnp.where(rises, up * px, down * (1 - px)), py)


def x_planes(came, valid):
    channels = valid.shape[2]
    data, flag = unpack(came, X_DATA, channels)
    xm = data[0 : 2 * PLANE].reshape(2, PLANE, channels) * valid
    cot = data[2 * PLANE :].astype(F32).reshape(1, PLANE, channels) * valid.astype(F32)
    return xm, cot, (1 - flag, flag)


def strips_body(spot_ref, xm_ref, cm_ref, xeven_ref, xodd_ref, fetched_ref, even_ref, odd_ref):
    px, py = spot(spot_ref)
    channels = xm_ref.shape[1]
    one = jnp.ones((1, 1, channels), BF)
    own_at = ((1 - py).reshape(1, 1, channels), py.reshape(1, 1, channels))
    xlow, xhigh = sides(xeven_ref, xodd_ref, "gx")
    xl, cl, at_l = x_planes(xlow, one)
    xh, ch, at_h = x_planes(xhigh, one)
    own = xm_ref[...].reshape(BE, PLANE, channels)
    cot = cm_ref[...].astype(F32).reshape(BE, PLANE, channels)
    strips = []
    for side in (0, 1):
        rows = slice(PLANE - 16, PLANE) if side else slice(0, 16)
        line = slice(PLANE - BE, PLANE) if side else slice(0, BE)
        lines = jnp.concatenate(
            [
                cl[:, line] * at_l[side].astype(F32),
                cot[:, line] * own_at[side].astype(F32),
                ch[:, line] * at_h[side].astype(F32),
            ],
            axis=0,
        )
        strip = [xl[:, rows] * at_l[side], own[:, rows] * own_at[side], xh[:, rows] * at_h[side]]
        strip = jnp.concatenate(strip, axis=0).reshape(Y_XM, channels)
        strips.append(jnp.concatenate([strip, lines.reshape(Y_COT, channels).astype(BF)], axis=0))
    place = lax.axis_index("gy") & 1
    pack(even_ref, jnp.where(place == 0, strips[1], strips[0]), px)
    pack(odd_ref, jnp.where(place == 1, strips[1], strips[0]), px)


def y_rows(came, px, channels):
    data, flag = unpack(came, Y_DATA, channels)
    strip = data[0:Y_XM].reshape(12, 16, channels)
    lines = data[Y_XM:].astype(F32).reshape(10, BE, channels)
    zero_at, one_at = 1 - flag, flag
    here_high = px.reshape(1, 1, channels)
    here_low = 1 - here_high
    same = zero_at * here_low + one_at * here_high
    xm = jnp.concatenate(
        [
            strip[0:2] * here_low + strip[8:10] * (zero_at * here_high),
            strip[2:10] * same,
            strip[10:12] * here_high + strip[2:4] * (one_at * here_low),
        ],
        axis=0,
    )
    f = lambda v: v.astype(F32)
    cot = jnp.concatenate(
        [
            lines[0:1] * f(here_low) + lines[8:9] * f(zero_at * here_high),
            lines[1:9] * f(same),
            lines[9:10] * f(here_high) + lines[1:2] * f(one_at * here_low),
        ],
        axis=0,
    )
    return xm, cot


def window_body(spot_ref, xm_ref, cm_ref, xeven_ref, xodd_ref, yeven_ref, yodd_ref, even_ref, odd_ref, cot_ref):
    px, py = spot(spot_ref)
    channels = xm_ref.shape[1]
    f = lambda v: v.astype(F32)
    high_x, high_y = px.reshape(1, 1, channels), py.reshape(1, 1, channels)
    low_x, low_y = 1 - high_x, 1 - high_y
    xlow, xhigh = sides(xeven_ref, xodd_ref, "gx")
    xl, cl, at_l = x_planes(xlow, low_x)
    xh, ch, at_h = x_planes(xhigh, high_x)
    ylow, yhigh = sides(yeven_ref, yodd_ref, "gy")
    sl, tl = y_rows(ylow, px, channels)
    sh, th = y_rows(yhigh, px, channels)
    own = xm_ref[...].reshape(BE, PLANE, channels)
    cot = cm_ref[...].astype(F32).reshape(BE, PLANE, channels)
    same_l = at_l[0] * low_y + at_l[1] * high_y
    same_h = at_h[0] * low_y + at_h[1] * high_y
    none8 = jnp.zeros((BE, 16, channels), BF)
    own_low = jnp.concatenate([xl[:, 48:64] * at_l[0], none8, xh[:, 48:64] * at_h[0]], axis=0)
    own_high = jnp.concatenate([xl[:, 0:16] * at_l[1], none8, xh[:, 0:16] * at_h[1]], axis=0)
    below = sl * low_y + own_low * high_y
    above = sh * high_y + own_high * low_y
    mid = jnp.concatenate([xl * same_l, own, xh * same_h], axis=0)
    even_ref[:, 0:16] = below
    even_ref[:, 16:80] = mid
    even_ref[:, 80:96] = above
    odd_ref[...] = jnp.concatenate([f(below)[:, 8:16], f(mid), f(above)[:, 0:8]], axis=1).astype(BF)
    none8 = jnp.zeros((BE, BE, channels), F32)
    cot_low = jnp.concatenate([cl[:, 56:64] * f(at_l[0]), none8, ch[:, 56:64] * f(at_h[0])], axis=0)
    cot_high = jnp.concatenate([cl[:, 0:8] * f(at_l[1]), none8, ch[:, 0:8] * f(at_h[1])], axis=0)
    cot_below = tl * f(low_y) + cot_low * f(high_y)
    cot_above = th * f(high_y) + cot_high * f(low_y)
    cot_mid = jnp.concatenate([cl * f(same_l), cot, ch * f(same_h)], axis=0)
    cot_ref[...] = jnp.concatenate([cot_below, cot_mid, cot_above], axis=1).astype(BF)


WIDE = 896


def z_shift(values, by):
    moved = pltpu.roll(values, by % BE, 1)
    place = lax.broadcasted_iota(jnp.int32, values.shape, 1)
    keep = place >= by if by > 0 else place < BE + by
    return jnp.where(keep, moved, 0.0)


def fetch_body(w_hbm, out_ref, done_ref, sem):
    copies = [
        pltpu.make_async_copy(w_hbm.at[pl.ds(9 * k, 9)], out_ref.at[pl.ds(9 * k, 9)], sem.at[k])
        for k in range(3)
    ]
    for copy in copies:
        copy.start()
    for copy in copies:
        copy.wait()
    done_ref[...] = jnp.zeros_like(done_ref)


def forward_body(parts, even_ref, odd_ref, cot_ref, w_ref, act_ref, slope_ref, *refs):
    channels = even_ref.shape[2]
    rows_refs, wide_ref = refs[:-1], refs[-1]
    me = lax.axis_index("gx")
    slots = 5

    def taken(first, a, b):
        some = slice(a + first, a + first + slots)
        piece = odd_ref[some] if b == 1 else even_ref[some, 8 * b : 8 * b + 80]
        return piece.reshape(80 * slots, channels)

    for first in range(0, 10, slots):
        columns = [taken(first, a, b) for a in range(3) for b in range(3)]
        columns = jnp.concatenate(columns, axis=1)
        pre = None
        for c in range(3):
            taps = jnp.concatenate([w_ref[3 * ab + c] for ab in range(9)], axis=1)
            total = lax.dot_general(columns, taps, NT, preferred_element_type=F32)
            total = total.reshape(10 * slots, BE, channels)
            if c != 1:
                total = z_shift(total, 1 - c)
            pre = total if pre is None else pre + total
        sigma = 1.0 / (1.0 + jnp.exp(-pre))
        cot = cot_ref[first : first + slots].astype(F32).reshape(10 * slots, BE, channels)
        slope = cot * (sigma * (1.0 + pre * (1.0 - sigma)))
        slope_ref[first : first + slots] = slope.reshape(slots, 80, channels).astype(BF)
        wide_ref[first : first + slots] = (pre * sigma).reshape(slots, 80, channels)
    act_ref[...] = wide_ref[1:9, 8:72].reshape(VOX, channels).astype(BF)
    block = channels // parts
    row = lax.broadcasted_iota(jnp.int32, (channels, channels), 0)
    col = lax.broadcasted_iota(jnp.int32, (channels, channels), 1)
    wanted = jnp.zeros_like(row)
    for k in range(parts):
        start = block * lax.bitwise_xor(me, jnp.int32(k))
        wanted = jnp.where(row >= block * k, row - block * k + start, wanted)
    pick = (col == wanted).astype(F32).astype(BF)
    slope = slope_ref[...].reshape(800, channels)
    lines = lax.dot_general(pick, slope, NT, preferred_element_type=F32).astype(BF)
    for k in range(parts):
        rows_refs[k][:, 0:800] = lines[block * k : block * (k + 1)]
        rows_refs[k][:, 800:] = jnp.zeros((block, WIDE - 800), BF)


def window_forward_body(parts, *refs):
    halo, w_ref, outs, scratch = refs[:7], refs[7], refs[9:-4], refs[-4:]
    windows, wide_ref = scratch[:3], scratch[3]
    window_body(*halo, *windows)
    forward_body(parts, *windows, w_ref, *outs, wide_ref)


def backward_body(slope_ref, act_ref, occ_ref, w_ref, out_ref, grad_ref):
    channels = slope_ref.shape[2]
    live = occ_ref[...].astype(F32)
    out_ref[...] = (act_ref[...].astype(F32).T * live).astype(BF)
    slope = slope_ref[...]
    middle = slope.astype(F32)[:, 8:72].astype(BF)
    columns = []
    for a in range(3):
        for b in range(3):
            if b == 1:
                piece = middle[2 - a : 10 - a]
            else:
                piece = slope[2 - a : 10 - a, 8 * (2 - b) : 8 * (2 - b) + 64]
            columns.append(piece.reshape(VOX, channels))
    columns = jnp.concatenate(columns, axis=1)
    grad = None
    for c in range(3):
        taps = jnp.concatenate([w_ref[3 * ab + c] for ab in range(9)], axis=0)
        total = jnp.dot(columns, taps, preferred_element_type=F32)
        total = total.reshape(PLANE, BE, channels)
        if c != 1:
            total = z_shift(total, c - 1)
        grad = total if grad is None else grad + total
    grad_ref[...] = (grad.reshape(VOX, channels).T * live).astype(BF)


def packing(width):
    full = width // 128
    rest = width - 128 * full
    per = 128 // rest if rest else 0
    return full, rest, per, 9 * full + (-(-9 // per) if rest else 0)


def folds(width, rows):
    _, rest, per, _ = packing(width)
    return bool(rest) and 9 % per == 1 and rows % 8 == 0 and rows // 8 * rest <= 128


def lines_of(width, rows):
    slots = packing(width)[3]
    used = (slots - 1) * rows + 8 if folds(width, rows) else slots * rows
    return -(-used // 16) * 16


def kernel_grad_body(last, chips, *refs):
    brick_ref, line_ref = refs[:2]
    outs = refs[2:]
    before = None
    if outs[0].shape[0] == 9 and len(outs) > 1:
        before, outs = outs[0], outs[1:]
    channels = brick_ref.shape[0]
    block = line_ref.shape[0]
    width = 3 * block
    place = lax.broadcasted_iota(jnp.int32, (block, WIDE), 1) & (BE - 1)
    g = line_ref[...].astype(F32)
    back = jnp.where(place < BE - 1, pltpu.roll(g, WIDE - 1, 1), 0.0)
    ahead = jnp.where(place > 0, pltpu.roll(g, 1, 1), 0.0)
    columns = jnp.concatenate([back, g, ahead], axis=0).astype(BF).T[0:800].reshape(10, 80, width)
    window, middle = columns, columns.astype(F32)[:, 8:72].astype(BF)
    left = brick_ref[...]
    full, rest, per, slots = packing(width)
    leftover = []
    store = outs[-1]
    for a in range(3):
        for b in range(3):
            if b == 1:
                piece = middle[2 - a : 10 - a]
            else:
                piece = window[2 - a : 10 - a, 8 * (2 - b) : 8 * (2 - b) + 64]
            total = jnp.dot(left, piece.reshape(VOX, width), preferred_element_type=F32)
            if before is not None:
                total = total + before[3 * a + b]
            if not last:
                store[3 * a + b] = total
                continue
            for n in range(full):
                store[(3 * a + b) * full + n] = total[:, 128 * n : 128 * n + 128]
            if rest:
                leftover.append(total[:, 128 * full :])
    if not last:
        return
    if rest:
        for n in range(slots - 9 * full):
            some = leftover[n * per : (n + 1) * per]
            spare = 128 - rest * len(some)
            if spare:
                some = some + [jnp.zeros((channels, spare), F32)]
            store[9 * full + n] = jnp.concatenate(some, axis=1)
    if len(outs) == 1:
        return
    send_ref, keep_ref, _ = outs
    rows = channels // (2 * chips)
    count = lines_of(width, rows)
    fold = folds(width, rows)
    core = lax.axis_index("gy") & 1
    for chip in range(chips):
        for whose, out in ((1 - core, send_ref), (core, keep_ref)):
            start = pl.multiple_of(rows * (2 * chip + whose), 8)
            piece = store[:, pl.ds(start, rows), :]
            if fold:
                tail = [piece[slots - 1, n : n + 8, :rest] for n in range(0, rows, 8)]
                tail.append(jnp.zeros((8, 128 - rest * len(tail)), F32))
                pieces = [piece[: slots - 1].reshape((slots - 1) * rows, 128), jnp.concatenate(tail, axis=1)]
            else:
                pieces = [piece.reshape(slots * rows, 128)]
            used = sum(part.shape[0] for part in pieces)
            if count > used:
                pieces.append(jnp.zeros((count - used, 128), F32))
            out[chip] = jnp.concatenate(pieces, axis=0).astype(out.dtype)


def pair_body(chips, keep_ref, recv_ref, own_ref, *send_refs):
    me = lax.axis_index("gy") >> 1
    own_ref[...] = keep_ref[me] + recv_ref[me].astype(F32)
    for k in range(1, chips):
        it = lax.bitwise_xor(me, jnp.int32(k))
        send_refs[k - 1][...] = (keep_ref[it] + recv_ref[it].astype(F32)).astype(BF)


def last_body(slots, width, scale, *refs):
    out_hbm, out_ref, sems = refs[-3:]
    copies = []
    total = refs[0][...]
    for other in refs[1:-3]:
        total = total + other[...].astype(F32)
    total = total * scale
    rows, block = out_ref.shape[1], width // 3
    full, rest, per, _ = packing(width)
    for ab in range(9):
        parts = [total[rows * (ab * full + n) : rows * (ab * full + n + 1)] for n in range(full)]
        if rest:
            at = rows * (9 * full + ab // per)
            lane = rest * (ab % per)
            if ab == 8 and folds(width, rows):
                tail = [total[at : at + 8, rest * n : rest * (n + 1)] for n in range(rows // 8)]
                parts.append(jnp.concatenate(tail, axis=0))
            else:
                parts.append(total[at : at + rows, lane : lane + rest])
        line = parts[0] if len(parts) == 1 else jnp.concatenate(parts, axis=1)
        for c in range(3):
            out_ref[3 * ab + c] = line[:, block * c : block * (c + 1)]
        if ab % 3 == 2:
            some = pl.ds(3 * ab - 6, 9)
            copies.append(pltpu.make_async_copy(out_ref.at[some], out_hbm.at[some], sems.at[ab // 3]))
            copies[-1].start()
    for copy in copies:
        copy.wait()


def xor_step(value, axis, step):
    count = lax.axis_size(axis)
    return lax.ppermute(value, axis, [(i, i ^ step) for i in range(count)])


def swap_pairs(even, odd, axis):
    count = lax.axis_size(axis)
    later = [(i, i + 1) for i in range(1, count - 1, 2)]
    odd = lax.ppermute(odd, axis, later + [(j, i) for i, j in later])
    return xor_step(even, axis, 1), odd


def shards(features, occupancy, brick_pos, weight, cotangent):
    channels = features.shape[3]
    parts, line = lax.axis_size("gx"), lax.axis_size("gy")
    chips = line // 2
    block, rows = channels // parts, channels // line
    feat = features.reshape(channels, VOX)
    cot = cotangent.reshape(channels, VOX)
    occ = occupancy.reshape(1, VOX)
    taps = weight.transpose(1, 0, 2)

    brick, plain = shape((VOX, channels), BF), shape((channels, VOX), BF)
    face, strip = message(X_DATA, channels), message(Y_DATA, channels)
    xm, cm, masked, even, odd, place = call(
        prep_body,
        [brick, brick, plain, face, face, shape((32, channels), BF)],
        [brick_pos, feat, occ, cot],
        scratch=[
            pltpu.SMEM((1, 1, 1), jnp.int32),
            pltpu.VMEM((channels, VOX), BF),
            pltpu.VMEM((1, VOX), jnp.int32),
            pltpu.VMEM((channels, VOX), BF),
            pltpu.SemaphoreType.DMA((4,)),
        ],
        anywhere=(0,),
        far=(1, 2, 3),
        short=True,
    )
    xeven, xodd = swap_pairs(even, odd, "gx")
    first = parts - 1
    bricks = {0: masked, first: xor_step(masked, "gx", first)}
    taps, fetched = call(
        fetch_body,
        [shape(taps.shape, BF), shape((16, 128), BF)],
        [taps],
        scratch=[pltpu.SemaphoreType.DMA((3,))],
        flops=10**9,
        far=(0,),
    )
    even, odd = call(strips_body, [strip, strip], [place, xm, cm, xeven, xodd, fetched], short=True)
    even, odd, again = lax.optimization_barrier((even, odd, masked))
    yeven, yodd = swap_pairs(even, odd, "gy")
    for k in reversed(range(1, parts)):
        if k != first:
            bricks[k] = xor_step(again, "gx", k)
    flops = 2 * VOX * 27 * channels * channels
    act, slope, *lines = call(
        functools.partial(window_forward_body, parts),
        [brick, shape((10, 80, channels), BF), *[shape((block, WIDE), BF)] * parts],
        [place, xm, cm, xeven, xodd, yeven, yodd, taps, bricks[first]],
        scratch=[
            pltpu.VMEM((12, 96, channels), BF),
            pltpu.VMEM((12, 80, channels), BF),
            pltpu.VMEM((10, 80, channels), BF),
            pltpu.VMEM((10, 80, channels), F32),
        ],
        short=True,
    )
    others = {k: xor_step(lines[k], "gx", k) for k in reversed(range(1, parts))}
    others = [others[k] for k in range(1, parts)]
    output, x_grad = call(backward_body, [plain, plain], [slope, act, occ, taps], flops=flops)

    width = 3 * block
    slots = packing(width)[3]
    count = lines_of(width, rows)
    table = (slots, channels, 128)
    lines = [lines[0]] + others
    so_far = []
    order = [0, *reversed(range(1, parts))]
    for k in order:
        last = k == order[-1]
        body = functools.partial(kernel_grad_body, last, chips)
        ins = [bricks[k], lines[k], *so_far]
        if not last:
            so_far = call(body, [shape((9, channels, width), F32)], ins, flops=flops // parts)
    if rows % 8 == 0:
        send, keep = call(
            body,
            [shape((chips, count, 128), BF), shape((chips, count, 128), F32)],
            ins,
            scratch=[pltpu.VMEM(table, F32)],
            flops=flops // parts,
        )
    else:
        (store,) = call(body, [shape(table, F32)], ins, flops=flops // parts)
        store = store.reshape(slots, chips, 2, rows, 128).transpose(2, 1, 0, 3, 4)
        store = store.reshape(2, chips, slots * rows, 128)
        store = jnp.pad(store, ((0, 0), (0, 0), (0, count - slots * rows), (0, 0)))
        core = lax.axis_index("gy") & 1
        keep = lax.dynamic_index_in_dim(store, core, 0, False)
        send = lax.dynamic_index_in_dim(store, 1 - core, 0, False).astype(BF)
    recv = xor_step(send, "gy", 1)
    own, *sends = call(
        functools.partial(pair_body, chips),
        [shape((count, 128), F32), *[shape((count, 128), BF)] * (chips - 1)],
        [keep, recv],
    )
    came = [xor_step(sends[k - 1], "gy", 2 * k) for k in reversed(range(1, chips))]
    (w_grad,) = call(
        functools.partial(last_body, slots, width, 1.0 / (parts * line)),
        [shape((27, rows, block), F32)],
        [own] + came,
        scratch=[pltpu.VMEM((27, rows, block), F32), pltpu.SemaphoreType.DMA((3,))],
        out_space=pltpu.HBM,
    )
    return (
        output.reshape(features.shape),
        x_grad.reshape(features.shape),
        w_grad.transpose(2, 0, 1),
    )


def solution(mesh):
    placed = (
        P("gx", "gy", None, None, None),
        P("gx", "gy", None, None),
        P("gx", "gy", None),
        P(),
        P("gx", "gy", None, None, None),
    )
    return jax.shard_map(
        shards,
        mesh=mesh,
        in_specs=placed,
        out_specs=(
            P("gx", "gy", None, None, None),
            P("gx", "gy", None, None, None),
            P("gx", None, "gy"),
        ),
        check_vma=False,
    )
```
